512 devices in a mesh: gz: 16 (over z_hi, x), ta: 32 (over y, z_lo, core).
Axes of the slice: x: 4, y: 8, z: 8 (z_hi: 4, z_lo: 2; z = z_hi * 2 + z_lo), core: 2. Of those that a mesh axis runs over, the one named last changes fastest.
Arguments:
- low_modes: bfloat16 [16, 2, 4, 3, 64, 32, 256], P(None, None, None, None, 'ta', 'gz'), may hold values from -6 to 6
- gauge_links: float32 [4, 18, 64, 32, 256], P(None, None, 'ta', 'gz'), may hold values from -2.5 to 2.5
- photon: float32 [4, 64, 32, 256], P(None, 'ta', 'gz'), may hold values from -5 to 5
- charges: int32 [16], replicated, may hold values from -2 to 2, as said below
- window_start: int32 [1], replicated, may hold values from 0 to 63
Outputs:
- insert_one: float32 [2, 16, 16], replicated
- insert_two: float32 [2, 16, 16], replicated
- window_one: float32 [2, 16, 16], replicated
- window_two: float32 [2, 16, 16], replicated
The draws below stay inside these ranges and needn't reach their ends.
Inputs may be any that keep to these rules, and one draw needn't show every extreme that they name: `charges`: never 0.
All inputs are finite; a program needn't handle non-finite values.
Results may differ from the reference program's by a relative error of at most 0.0003.
Values may be sent and summed in bfloat16 or wider, within the bound.
A program may use at most 64 MiB of HBM per device.

```python
import math
import jax
import jax.numpy as jnp
import numpy as np
from jax import lax

MODES = 16
LY = 16
TW = 4
LXY = 256
NZ = 32
NT = 64


def draw_charges(key, part):
    key = jax.random.fold_in(key, 7)
    level = jax.random.randint(key, (MODES,), 0, 4)
    return (level - 2 + (level >= 2).astype(jnp.int32)).astype(jnp.int32)


def steps_of(key, dims, split, smallest, largest):
    def one(dim, parts):
        steps = jax.random.uniform(jax.random.fold_in(jax.random.fold_in(key, 6), dim), (parts,), jnp.float32, smallest / len(split), largest / len(split))
        return jnp.repeat(jnp.exp(steps), dims[dim] // parts).reshape((-1,) + (1,) * (len(dims) - dim - 1))

    loudness = one(*split[0])
    for cut in split[1:]:
        loudness = loudness * one(*cut)
    return loudness


def normal_values(key, dims, spread, bound, pieces=(), kind=jnp.bfloat16):
    loudness = steps_of(key, dims, pieces, -0.22, 0.18) if pieces else 1.0
    values = jax.random.normal(key, dims, jnp.float32) * spread * loudness
    return jnp.minimum(jnp.maximum(values, -bound), bound).astype(kind)


def setup_inputs(seed: int = 0) -> dict:
    keys = jax.random.split(jax.random.key(seed), 6)
    return {
        "low_modes": normal_values(keys[0], (MODES, 2, 4, 3, NT, NZ, LXY), 1.0, 6.0, ((4, 32), (5, 16))),
        "gauge_links": normal_values(keys[1], (4, 18, NT, NZ, LXY), 0.41, 2.5, ((2, 32), (3, 16)), jnp.float32),
        "photon": normal_values(keys[2], (4, NT, NZ, LXY), 1.0, 5.0, ((1, 32), (2, 16)), jnp.float32),
        "charges": draw_charges(jax.random.fold_in(keys[5], 71), 0),
        "window_start": jax.random.randint(keys[4], (1,), 0, NT).astype(jnp.int32),
    }


def gamma_tables():
    table_real = np.zeros((4, 4, 4))
    table_imag = np.zeros((4, 4, 4))
    table_imag[0, 0, 3] = 1.0
    table_imag[0, 1, 2] = 1.0
    table_imag[0, 2, 1] = -1.0
    table_imag[0, 3, 0] = -1.0
    table_real[1, 0, 3] = -1.0
    table_real[1, 1, 2] = 1.0
    table_real[1, 2, 1] = 1.0
    table_real[1, 3, 0] = -1.0
    table_imag[2, 0, 2] = 1.0
    table_imag[2, 1, 3] = -1.0
    table_imag[2, 2, 0] = -1.0
    table_imag[2, 3, 1] = 1.0
    table_real[3, 0, 2] = 1.0
    table_real[3, 1, 3] = 1.0
    table_real[3, 2, 0] = 1.0
    table_real[3, 3, 1] = 1.0
    return (table_real, table_imag)

def color_apply(link_data, values, adjoint):
    rows_real = []
    rows_imag = []
    for a in range(3):
        sum_real = 0.0
        sum_imag = 0.0
        for b in range(3):
            if adjoint:
                link_real = link_data[b * 3 + a]
                link_imag = -link_data[9 + b * 3 + a]
            else:
                link_real = link_data[a * 3 + b]
                link_imag = link_data[9 + a * 3 + b]
            part_real = values[:, 0, :, b]
            part_imag = values[:, 1, :, b]
            sum_real = sum_real + link_real * part_real - link_imag * part_imag
            sum_imag = sum_imag + link_real * part_imag + link_imag * part_real
        rows_real.append(sum_real)
        rows_imag.append(sum_imag)
    return jnp.stack([jnp.stack(rows_real, axis=2), jnp.stack(rows_imag, axis=2)], axis=1)

def spin_apply(direction, sign_factor, values):
    table_real, table_imag = gamma_tables()
    spins_real = []
    spins_imag = []
    for s in range(4):
        spin_real = values[:, 0, s]
        spin_imag = values[:, 1, s]
        for k in range(4):
            entry_real = sign_factor * float(table_real[direction, s, k])
            entry_imag = sign_factor * float(table_imag[direction, s, k])
            if entry_real != 0.0:
                spin_real = spin_real + entry_real * values[:, 0, k]
                spin_imag = spin_imag + entry_real * values[:, 1, k]
            if entry_imag != 0.0:
                spin_real = spin_real - entry_imag * values[:, 1, k]
                spin_imag = spin_imag + entry_imag * values[:, 0, k]
        spins_real.append(spin_real)
        spins_imag.append(spin_imag)
    return jnp.stack([jnp.stack(spins_real, axis=1), jnp.stack(spins_imag, axis=1)], axis=1)

def shift_xy(values, direction, in_front, last_y, first_y):
    if direction == 0:
        return jnp.roll(values, -LY if in_front else LY, axis=-1)
    if in_front:
        return jnp.where(last_y, jnp.roll(values, LY - 1, axis=-1), jnp.roll(values, -1, axis=-1))
    return jnp.where(first_y, jnp.roll(values, 1 - LY, axis=-1), jnp.roll(values, 1, axis=-1))

def insert_block(padded, padded_links, charge):
    values = padded.astype(jnp.float32)
    centre = values[:, :, :, :, 1:-1, 1:-1, :]
    link_mid = padded_links[:, :, 1:-1, 1:-1, :]
    sites_xy = centre.shape[-1]
    column = jnp.arange(sites_xy) % LY
    last_y = column == LY - 1
    first_y = column == 0
    first_order = jnp.zeros_like(centre)
    second_order = jnp.zeros_like(centre)
    for direction in range(4):
        if direction < 2:
            in_front = shift_xy(centre, direction, True, last_y, first_y)
            behind = shift_xy(centre, direction, False, last_y, first_y)
            link_behind = shift_xy(link_mid[direction], direction, False, last_y, first_y)
        elif direction == 2:
            in_front = values[:, :, :, :, 1:-1, 2:, :]
            behind = values[:, :, :, :, 1:-1, :-2, :]
            link_behind = padded_links[direction, :, 1:-1, :-2, :]
        else:
            in_front = values[:, :, :, :, 2:, 1:-1, :]
            behind = values[:, :, :, :, :-2, 1:-1, :]
            link_behind = padded_links[direction, :, :-2, 1:-1, :]
        link_here = link_mid[direction]
        forward = spin_apply(direction, -1.0, color_apply(link_here, in_front, False))
        backward = spin_apply(direction, 1.0, color_apply(link_behind, behind, True))
        photon_here = link_here[18]
        photon_behind = link_behind[18]
        difference = photon_here * forward - photon_behind * backward
        first_order = first_order + 0.5 * jnp.stack([difference[:, 1], -difference[:, 0]], axis=1)
        second_order = second_order + 0.25 * (photon_here * photon_here * forward + photon_behind * photon_behind * backward)
    charge_column = charge.reshape((-1, 1, 1, 1, 1, 1, 1))
    return (first_order * charge_column, second_order * charge_column * charge_column)

def contract_all(bra, ket):
    bra_rows = bra.reshape(bra.shape[0], 2, -1)
    ket_rows = ket.reshape(ket.shape[0], 2, -1)
    products = lax.dot_general(bra_rows, ket_rows, (((2,), (2,)), ((), ())), precision=lax.Precision.HIGHEST, preferred_element_type=jnp.float32)
    real_part = products[:, 0, :, 0] + products[:, 1, :, 1]
    imag_part = products[:, 0, :, 1] - products[:, 1, :, 0]
    return jnp.stack([real_part, imag_part])

def slab_matrices(values, links_slab, charge, bra):
    groups = MODES // 8
    stacked = values.reshape((groups, 8) + values.shape[1:])
    charge_groups = charge.reshape(groups, 8)

    def one_group(group_pair):
        first_order, second_order = insert_block(group_pair[0], links_slab, group_pair[1])
        return jnp.stack([contract_all(bra, first_order), contract_all(bra, second_order)])
    results = lax.map(one_group, (stacked, charge_groups))
    return jnp.transpose(results, (1, 2, 3, 0, 4)).reshape(2, 2, MODES, MODES)

def wrap_z(values, axis):
    extent = values.shape[axis]
    return jnp.concatenate([lax.slice_in_dim(values, extent - 1, extent, axis=axis), values, lax.slice_in_dim(values, 0, 1, axis=axis)], axis=axis)

def reference(low_modes, gauge_links, photon, charges, window_start):
    link_data = jnp.concatenate([gauge_links, photon[:, None]], axis=1)
    charge = charges.astype(jnp.float32) / 3.0
    start = window_start[0]

    def one_slab(totals, slab_time):
        earlier = (slab_time + NT - 1) % NT
        later = (slab_time + 1) % NT
        slab_rows = jnp.stack([earlier, slab_time, later]).astype(jnp.int32)
        values = jnp.take(low_modes, slab_rows, axis=4)
        low_sign = jnp.where(slab_time == 0, -1.0, 1.0)
        high_sign = jnp.where(slab_time == NT - 1, -1.0, 1.0)
        sign_rows = jnp.stack([low_sign, jnp.ones_like(low_sign), high_sign]).astype(low_modes.dtype)
        values = wrap_z(values * sign_rows[:, None, None], 5)
        links_slab = wrap_z(jnp.take(link_data, slab_rows, axis=2), 3)
        bra = lax.dynamic_slice_in_dim(low_modes, slab_time, 1, axis=4).astype(jnp.float32)
        mats = slab_matrices(values, links_slab, charge, bra)
        window_mask = ((slab_time - start) % NT < TW).astype(mats.dtype)
        return ((totals[0] + mats[0], totals[1] + mats[1], totals[2] + window_mask * mats[0], totals[3] + window_mask * mats[1]), None)
    zeros = jnp.zeros((2, MODES, MODES), jnp.float32)
    totals, _ = lax.scan(one_slab, (zeros, zeros, zeros, zeros), jnp.arange(NT, dtype=jnp.int32))
    main_scale = 1.0 / math.sqrt(24.0 * NT * NZ * LXY)
    window_scale = 1.0 / math.sqrt(24.0 * TW * NZ * LXY)
    return (totals[0] * main_scale, totals[1] * main_scale, totals[2] * window_scale, totals[3] * window_scale)
```

```python
import functools
import math

import jax
import jax.numpy as jnp
import numpy as np
from jax import lax
from jax.experimental import pallas as pl
from jax.experimental.pallas import tpu as pltpu
from jax.sharding import PartitionSpec as P

LY = 16
TW = 4
MODES = 16
SC = 12
SITES = 256
KETS = 192
MESH = pl.DeviceIdType.MESH

GAMMA = (
    ((3, 0, 1), (2, 0, 1), (1, 0, -1), (0, 0, -1)),
    ((3, -1, 0), (2, 1, 0), (1, 1, 0), (0, -1, 0)),
    ((2, 0, 1), (3, 0, -1), (0, 0, -1), (1, 0, 1)),
)


def fold_tables():
    space = np.zeros((2, 2, 128, 128), np.float32)
    time = np.zeros((2, 2, 2, 64, 128), np.float32)

    def put(table, column, half, mode, bra, ket, kind, sign):
        j = half * 8 + mode
        if bra == ket:
            table[column, kind * 16 + j] += sign
        elif bra == 0:
            table[column, 64 + kind * 16 + j] += sign
        else:
            table[column, 64 + kind * 16 + j] -= sign

    for bra in range(2):
        for half in range(2):
            for order in range(2):
                for part in range(2):
                    for ket in range(2):
                        for mode in range(8):
                            low = part * 16 + ket * 8 + mode
                            s_col = (order * 2) * 32 + low
                            d_col = (order * 2 + 1) * 32 + low
                            t_col = order * 32 + low
                            f, b = order * 2, order * 2 + 1
                            put(space[bra, half], s_col, half, mode, bra, ket, f, 1)
                            put(space[bra, half], s_col, half, mode, bra, ket, b, 1)
                            put(space[bra, half], d_col, half, mode, bra, ket, f, -1)
                            put(space[bra, half], d_col, half, mode, bra, ket, b, 1)
                            put(time[0, bra, half], t_col, half, mode, bra, ket, f, 1)
                            put(time[0, bra, half], t_col, half, mode, bra, ket, b, 1)
                            put(time[1, bra, half], t_col, half, mode, bra, ket, f, -1)
                            put(time[1, bra, half], t_col, half, mode, bra, ket, b, 1)
    return space.reshape(512, 128), time.reshape(512, 128)


def split(value):
    high = value.astype(jnp.bfloat16)
    low = (value - high.astype(jnp.float32)).astype(jnp.bfloat16)
    return high, low


def colour_row(rows, vectors):
    result = []
    for spin in range(4):
        total_re = None
        total_im = None
        for b in range(3):
            ur, ui = rows[b]
            value = vectors(spin * 3 + b)
            vr, vi = value[:8], value[8:]
            re = ur * vr - ui * vi
            im = ur * vi + ui * vr
            total_re = re if total_re is None else total_re + re
            total_im = im if total_im is None else total_im + im
        result.append((total_re, total_im))
    return result


def times(entry, pair):
    _, re, im = entry
    if re:
        return (re, pair[0]), (re, pair[1])
    return (-im, pair[1]), (im, pair[0])


def add_signed(total, sign, value):
    if total is None:
        return value if sign > 0 else -value
    return total + value if sign > 0 else total - value


def vector_unit(block_t, block_z, lane, half, vall, vxy, links, field, ket):
    rows16 = pl.ds(half * 16, 16)
    lanes = pl.ds(pl.multiple_of(lane * 128, 128), 128)
    lanes_y = pl.ds(pl.multiple_of(256 + lane * 128, 128), 128)

    def from_x(sc):
        return vxy[pl.ds(sc * 32 + half * 16, 16), lanes]

    def from_y(sc):
        return vxy[pl.ds(sc * 32 + half * 16, 16), lanes_y]

    def from_z(sc):
        return vall[block_t, block_z + 1, sc, rows16, lanes].astype(jnp.float32)

    def from_t(sc):
        return vall[block_t + 1, block_z, sc, rows16, lanes].astype(jnp.float32)

    sources = (from_x, from_y, from_z, from_t)

    def store(kind_row, sc, pair):
        high, low = split(jnp.concatenate(pair, axis=0))
        ket[pl.ds(kind_row, 16), pl.ds(sc * 128, 128)] = high
        ket[pl.ds(kind_row + 16, 16), pl.ds(sc * 128, 128)] = low

    for a in range(3):
        sums = [[[None, None] for _ in range(4)] for _ in range(4)]
        for mu in range(4):
            rows = [
                (
                    links[block_t, block_z, mu * 18 + a * 3 + b, :, lanes],
                    links[block_t, block_z, mu * 18 + 9 + a * 3 + b, :, lanes],
                )
                for b in range(3)
            ]
            photon = field[block_t, block_z, mu, :, lanes]
            first = colour_row(rows, sources[mu])
            second = [(photon * re, photon * im) for re, im in first]
            if mu == 3:
                for spin in range(4):
                    store(128, spin * 3 + a, first[spin])
                    store(160, spin * 3 + a, second[spin])
                continue
            for order, hopped in enumerate((first, second)):
                for spin in range(4):
                    plain = sums[order * 2][spin]
                    crossed = sums[order * 2 + 1][spin]
                    entry = GAMMA[mu][spin]
                    turned = times(entry, hopped[entry[0]])
                    for part in range(2):
                        plain[part] = add_signed(plain[part], 1, hopped[spin][part])
                        crossed[part] = add_signed(crossed[part], *turned[part])
        for kind in range(4):
            for spin in range(4):
                store(kind * 32, spin * 3 + a, sums[kind][spin])


def product_unit(block_t, block_z, lane, half, vall, ket, acc):
    lanes = pl.ds(pl.multiple_of(lane * 128, 128), 128)
    pieces = [vall[block_t, block_z, sc, :, lanes] for sc in range(SC)]
    bra = jnp.concatenate(
        [
            jnp.concatenate(pieces, axis=1),
            jnp.concatenate(pieces[6:] + pieces[:6], axis=1),
        ],
        axis=0,
    )
    acc[block_t, half] += lax.dot_general(
        bra, ket[...], (((1,), (1,)), ((), ())), preferred_element_type=jnp.float32
    )


def hop_kernel(
    counts,
    comm,
    start_ref,
    low_ref,
    link_ref,
    photon_ref,
    space_ref,
    time_ref,
    out_ref,
    vall,
    vxy,
    perm,
    links,
    field,
    ket_a,
    ket_b,
    acc,
    slots,
    local_sem,
    send_sem,
    recv_sem,
    sum_send,
    sum_recv,
):
    n_gz, n_ta = counts
    if comm:
        gz, ta = lax.axis_index("gz"), lax.axis_index("ta")
    else:
        gz, ta = 0, 0

    def at(g, t):
        return {"gz": g, "ta": t}

    z_hi, x = gz // 4, gz % 4
    y, z_lo, core = ta // 4, (ta // 2) % 2, ta % 2
    z = z_hi * 2 + z_lo

    def group_a(index):
        return at(z_hi * 4 + index // 2, y * 4 + z_lo * 2 + index % 2)

    def group_b(index):
        return at((index // 2) * 4 + x, y * 4 + (index % 2) * 2 + core)

    def group_c(index):
        return at(gz, index * 4 + z_lo * 2 + core)

    stages = ((group_a, x * 2 + core), (group_b, z), (group_c, y))
    below_z = at((gz + n_gz - 1) % n_gz, ta)
    above_z = at((gz + 1) % n_gz, ta)
    below_t = at(gz, (ta + n_ta - 1) % n_ta)
    above_t = at(gz, (ta + 1) % n_ta)

    barrier = pltpu.get_barrier_semaphore() if comm else None
    if comm:
        for device in (below_z, above_z, below_t, above_t):
            pl.semaphore_signal(barrier, inc=1, device_id=device, device_id_type=MESH)
        for group, index in stages:
            for step in range(1, 8):
                pl.semaphore_signal(
                    barrier, inc=1, device_id=group((index + step) % 8), device_id_type=MESH
                )

    own = [
        pltpu.make_async_copy(low_ref.at[t, zz], vall.at[t, zz], local_sem.at[t * 2 + zz])
        for t in range(2)
        for zz in range(2)
    ]
    for copy in own:
        copy.start()

    def halo(src, dst, which, device):
        if comm:
            return pltpu.make_async_remote_copy(
                src_ref=low_ref.at[src],
                dst_ref=vall.at[dst],
                send_sem=send_sem.at[which],
                recv_sem=recv_sem.at[which],
                device_id=device,
                device_id_type=MESH,
            )
        return pltpu.make_async_copy(low_ref.at[src], vall.at[dst], recv_sem.at[which])

    halos = [
        halo((0, 0), (2, 0), 0, below_t),
        halo((0, 0), (0, 2), 1, below_z),
        halo((0, 1), (2, 1), 2, below_t),
        halo((1, 0), (1, 2), 3, below_z),
    ]

    if comm:
        pl.semaphore_wait(barrier, 25)
    for copy in halos:
        copy.start()

    row = lax.broadcasted_iota(jnp.int32, (SITES, SITES), 0)
    column = lax.broadcasted_iota(jnp.int32, (SITES, SITES), 1)
    along_x = (column + LY) % SITES
    along_y = (column - column % LY) + (column + 1) % LY
    perm[:, :SITES] = (row == along_x).astype(jnp.float32).astype(jnp.bfloat16)
    perm[:, SITES:] = (row == along_y).astype(jnp.float32).astype(jnp.bfloat16)

    def spread(t, _):
        edge = jnp.where(jnp.logical_and(ta == n_ta - 1, t == 1), -1.0, 1.0)
        for mu in range(4):
            photon = photon_ref[mu, t]
            scale = photon * edge if mu == 3 else photon
            for zz in range(2):
                field[t, zz, mu] = jnp.broadcast_to(photon[zz : zz + 1], (8, SITES))
            for entry in range(18):
                scaled = link_ref[mu, entry, t] * scale
                for zz in range(2):
                    links[t, zz, mu * 18 + entry] = jnp.broadcast_to(
                        scaled[zz : zz + 1], (8, SITES)
                    )
        return 0

    lax.fori_loop(0, 2, spread, 0)

    acc[...] = jnp.zeros_like(acc)
    ket_b[...] = jnp.zeros_like(ket_b)
    for copy in own:
        copy.wait()

    def step(index, _):
        block = index // 2
        lane = index % 2
        block_t, block_z = block % 2, block // 2
        before = jnp.maximum(index - 1, 0)
        before_block = before // 2
        before_t, before_z, before_lane = before_block % 2, before_block // 2, before % 2

        @pl.when(lane == 0)
        def _():
            for which, number in ((0, 1), (1, 2), (2, 3), (3, 3)):
                @pl.when(block == number)
                def _(which=which):
                    halos[which].wait_recv() if comm else halos[which].wait()

            vxy[...] = jnp.dot(
                vall[block_t, block_z].reshape(SC * 32, SITES),
                perm[...],
                preferred_element_type=jnp.float32,
            )

        product_unit(before_t, before_z, before_lane, 1, vall, ket_b, acc)
        vector_unit(block_t, block_z, lane, 0, vall, vxy, links, field, ket_a)
        product_unit(block_t, block_z, lane, 0, vall, ket_a, acc)
        vector_unit(block_t, block_z, lane, 1, vall, vxy, links, field, ket_b)
        return 0

    lax.fori_loop(0, 8, step, 0)
    product_unit(1, 1, 1, 1, vall, ket_b, acc)

    def bra_rows(values, swapped, part):
        base = swapped * 32 + part * 8
        return jnp.concatenate([values[base : base + 8], values[base + 16 : base + 24]], axis=0)

    total = jnp.zeros((MODES, 128), jnp.float32)
    inside_total = jnp.zeros((MODES, 128), jnp.float32)
    lattice_t = 2 * n_ta
    begin = start_ref[0]
    kind = lax.broadcasted_iota(jnp.int32, (1, 128), 1) // 16 % 2

    def inside(t):
        offset = (t - begin + 2 * lattice_t) % lattice_t
        return jnp.where(offset < TW, 1.0, 0.0)

    for t in range(2):
        space_sum = jnp.zeros((MODES, 128), jnp.float32)
        time_sum = jnp.zeros((MODES, 128), jnp.float32)
        for half in range(2):
            values = acc[t, half]
            for part in range(2):
                table = space_ref[pl.ds((part * 2 + half) * 128, 128), :]
                space_sum += jnp.dot(
                    bra_rows(values, 0, part)[:, :128],
                    table,
                    precision=lax.Precision.HIGHEST,
                    preferred_element_type=jnp.float32,
                )
                for swapped in range(2):
                    table = time_ref[pl.ds(((swapped * 2 + part) * 2 + half) * 64, 64), :]
                    time_sum += jnp.dot(
                        bra_rows(values, swapped, part)[:, 128:],
                        table,
                        precision=lax.Precision.HIGHEST,
                        preferred_element_type=jnp.float32,
                    )
        here = inside(ta * 2 + t)
        after = inside(ta * 2 + t + 1)
        total += space_sum + time_sum
        inside_total += here * space_sum + jnp.where(kind == 0, here, after) * time_sum

    value = jnp.concatenate([total, inside_total], axis=0)
    if comm:
        for number, (group, index) in enumerate(stages):
            slots[number, index] = value
            copies = []
            for hop in range(1, 8):
                copy = pltpu.make_async_remote_copy(
                    src_ref=slots.at[number, index],
                    dst_ref=slots.at[number, index],
                    send_sem=sum_send.at[number, hop],
                    recv_sem=sum_recv.at[number, index],
                    device_id=group((index + hop) % 8),
                    device_id_type=MESH,
                )
                copy.start()
                copies.append(copy)
            for hop in range(1, 8):
                peer = (index + hop) % 8
                pltpu.make_async_remote_copy(
                    src_ref=slots.at[number, peer],
                    dst_ref=slots.at[number, peer],
                    send_sem=sum_send.at[number, hop],
                    recv_sem=sum_recv.at[number, peer],
                    device_id=group(peer),
                    device_id_type=MESH,
                ).wait_recv()
            value = slots[number, 0]
            for other in range(1, 8):
                value = value + slots[number, other]
            for copy in copies:
                copy.wait_send()
        for copy in halos:
            copy.wait_send()
    out_ref[...] = value.reshape(2, MODES, 128)


def insert_sums(counts, comm, low, links, photon, start):
    space, time = fold_tables()
    vmem = pl.BlockSpec(memory_space=pltpu.VMEM)
    return pl.pallas_call(
        functools.partial(hop_kernel, counts, comm),
        out_shape=jax.ShapeDtypeStruct((2, MODES, 128), jnp.float32),
        in_specs=[
            pl.BlockSpec(memory_space=pltpu.SMEM),
            pl.BlockSpec(memory_space=pl.ANY),
            vmem,
            vmem,
            vmem,
            vmem,
        ],
        out_specs=vmem,
        scratch_shapes=[
            pltpu.VMEM((3, 3, SC, 32, SITES), jnp.bfloat16),
            pltpu.VMEM((SC * 32, 2 * SITES), jnp.float32),
            pltpu.VMEM((SITES, 2 * SITES), jnp.bfloat16),
            pltpu.VMEM((2, 2, 72, 8, SITES), jnp.float32),
            pltpu.VMEM((2, 2, 4, 8, SITES), jnp.float32),
            pltpu.VMEM((KETS, SC * 128), jnp.bfloat16),
            pltpu.VMEM((KETS, SC * 128), jnp.bfloat16),
            pltpu.VMEM((2, 2, 64, KETS), jnp.float32),
            pltpu.VMEM((3, 8, 2 * MODES, 128), jnp.float32),
            pltpu.SemaphoreType.DMA((4,)),
            pltpu.SemaphoreType.DMA((4,)),
            pltpu.SemaphoreType.DMA((4,)),
            pltpu.SemaphoreType.DMA((3, 8)),
            pltpu.SemaphoreType.DMA((3, 8)),
        ],
        compiler_params=pltpu.CompilerParams(
            collective_id=0 if comm else None,
            has_side_effects=comm,
            vmem_limit_bytes=32 * 1024 * 1024,
        ),
    )(start, low, links, photon, jnp.asarray(space), jnp.asarray(time))


def per_device(counts, comm, low_modes, gauge_links, photon, charges, window_start):
    n_gz, n_ta = counts
    low = low_modes.reshape(2, 8, 2, SC, 2, 2, SITES)
    low = low.transpose(4, 5, 3, 0, 2, 1, 6).reshape(2, 2, SC, 32, SITES)
    sums = insert_sums(counts, comm, low, gauge_links, photon, window_start)
    sums = sums.reshape(2, MODES, 2, 4, MODES)
    charge = charges.astype(jnp.float32) / 3.0
    lattice = 24.0 * SITES * (2 * n_gz)
    scales = (1.0 / math.sqrt(lattice * 2 * n_ta), 1.0 / math.sqrt(lattice * TW))
    outputs = []
    for window in range(2):
        for order in range(2):
            f_re = sums[window, :, 0, 2 * order]
            f_im = sums[window, :, 1, 2 * order]
            b_re = sums[window, :, 0, 2 * order + 1].T
            b_im = -sums[window, :, 1, 2 * order + 1].T
            if order == 0:
                factor = 0.5 * scales[window] * charge
                outputs.append(jnp.stack([(f_im - b_im) * factor, -(f_re - b_re) * factor]))
            else:
                factor = 0.25 * scales[window] * charge * charge
                outputs.append(jnp.stack([(f_re + b_re) * factor, (f_im + b_im) * factor]))
    return tuple(outputs)


def solution(mesh):
    counts = (mesh.shape["gz"], mesh.shape["ta"])
    return jax.shard_map(
        functools.partial(per_device, counts, True),
        mesh=mesh,
        in_specs=(
            P(None, None, None, None, "ta", "gz", None),
            P(None, None, "ta", "gz", None),
            P(None, "ta", "gz", None),
            P(),
            P(),
        ),
        out_specs=(P(), P(), P(), P()),
        check_vma=False,
    )
```

```python
import functools
import math

import jax
import jax.numpy as jnp
import numpy as np
from jax import lax
from jax.experimental import pallas as pl
from jax.experimental.pallas import tpu as pltpu
from jax.sharding import PartitionSpec as P

LY = 16
TW = 4
MODES = 16
SC = 12
SITES = 256
ROWS = SC * 32
EDGE = 24
MESH = pl.DeviceIdType.MESH

GAMMA = (
    ((3, 0, 1), (2, 0, 1), (1, 0, -1), (0, 0, -1)),
    ((3, -1, 0), (2, 1, 0), (1, 1, 0), (0, -1, 0)),
    ((2, 0, 1), (3, 0, -1), (0, 0, -1), (1, 0, 1)),
)


def fold_table():
    table = np.zeros((1536, 128), np.float32)

    def put(row, ket, order, plain, value):
        for side in range(2):
            factor = value * (0.5 if order == 0 else 0.25)
            if side == 0:
                factor = factor if plain else -factor
                factor = factor * (-1j if order == 0 else 1)
                parts = (factor.real, factor.imag)
            else:
                factor = np.conj(factor) * (1j if order == 0 else 1)
                parts = (factor.real, factor.imag)
            for part in range(2):
                table[row, side * 64 + part * 32 + order * 16 + ket] += parts[part]

    for bra in range(2):
        for half in range(2):
            for low in range(2):
                for part in range(2):
                    for mode in range(8):
                        ket = half * 8 + mode
                        value = (1, -1j)[bra] * (1, 1j)[part]
                        tail = low * 16 + part * 8 + mode
                        for kind in range(4):
                            row = bra * 256 + half * 128 + kind * 32 + tail
                            put(row, ket, kind // 2, kind % 2 == 0, value)
                        for order in range(2):
                            for turned in range(2):
                                row = (turned * 2 + bra) * 128 + half * 64 + order * 32 + tail
                                put(512 + row, ket, order, turned == 0, value)
                                phase = 1j if turned else 1
                                put(1024 + row, ket, order, turned == 0, value * phase)
    return table


def split(value):
    high = value.astype(jnp.bfloat16)
    low = (value - high.astype(jnp.float32)).astype(jnp.bfloat16)
    return high, low


def colour_row(rows, vectors):
    result = []
    for spin in range(4):
        total_re = None
        total_im = None
        for b in range(3):
            ur, ui = rows[b]
            value = vectors(spin * 3 + b)
            vr, vi = value[:8], value[8:]
            re = ur * vr - ui * vi
            im = ur * vi + ui * vr
            total_re = re if total_re is None else total_re + re
            total_im = im if total_im is None else total_im + im
        result.append((total_re, total_im))
    return result


def times(entry, pair):
    _, re, im = entry
    if re:
        return (re, pair[0]), (re, pair[1])
    return (-im, pair[1]), (im, pair[0])


def add_signed(total, sign, value):
    if total is None:
        return value if sign > 0 else -value
    return total + value if sign > 0 else total - value


def link_rows(links, slot, base, a, lanes):
    return [
        (links[slot, base + a * 3 + b, :, lanes], links[slot, base + 9 + a * 3 + b, :, lanes])
        for b in range(3)
    ]


def store_pair(ket, row, column, pair):
    high, low = split(jnp.concatenate(pair, axis=0))
    ket[row : row + 16, column : column + 128] = high
    ket[row + 16 : row + 32, column : column + 128] = low


def space_unit(t, zz, lane, half, vall, vxy, links, field, ket):
    lanes = slice(lane * 128, lane * 128 + 128)
    slot = t * 2 + zz

    def from_x(sc):
        return vxy[sc * 32 + half * 16 : sc * 32 + half * 16 + 16, lanes]

    def from_y(sc):
        row = sc * 32 + half * 16
        return vxy[row : row + 16, SITES + lane * 128 : SITES + lane * 128 + 128]

    def from_z(sc):
        rows = slice(half * 16, half * 16 + 16)
        return vall[t + 1, zz + 2, sc, rows, lanes].astype(jnp.float32)

    sources = (from_x, from_y, from_z) if zz == 0 else (from_x, from_y)
    for a in range(3):
        sums = [[[None, None] for _ in range(4)] for _ in range(4)]
        for mu, source in enumerate(sources):
            first = colour_row(link_rows(links, slot, mu * 18, a, lanes), source)
            photon = field[slot, mu, :, lanes]
            second = [(photon * re, photon * im) for re, im in first]
            for order, hopped in enumerate((first, second)):
                for spin in range(4):
                    plain = sums[order * 2][spin]
                    crossed = sums[order * 2 + 1][spin]
                    entry = GAMMA[mu][spin]
                    turned = times(entry, hopped[entry[0]])
                    for part in range(2):
                        plain[part] = add_signed(plain[part], 1, hopped[spin][part])
                        crossed[part] = add_signed(crossed[part], *turned[part])
        for kind in range(4):
            for spin in range(4):
                store_pair(ket, half * 128 + kind * 32, (spin * 3 + a) * 128, sums[kind][spin])


def space_product(t, zz, lane, vall, ket):
    lanes = slice(lane * 128, lane * 128 + 128)
    bra = jnp.concatenate([vall[t + 1, zz + 1, sc, :, lanes] for sc in range(SC)], axis=1)
    return lax.dot_general(
        bra, ket[...], (((1,), (1,)), ((), ())), preferred_element_type=jnp.float32
    )


def link_unit(up, slot, mu, lane, half, vall, links, field, ket):
    lanes = slice(lane * 128, lane * 128 + 128)

    def source(sc):
        return vall[up[0], up[1], sc, half * 16 : half * 16 + 16, lanes].astype(jnp.float32)

    photon = field[slot, mu, :, lanes]
    for a in range(3):
        first = colour_row(link_rows(links, slot, mu * 18, a, lanes), source)
        for spin in range(4):
            re, im = first[spin]
            column = (spin * 3 + a) * SITES + lane * 128
            store_pair(ket, half * 64, column, (re, im))
            store_pair(ket, half * 64 + 32, column, (photon * re, photon * im))


def link_product(low, sign, vall, ket):
    pieces = [vall[low[0], low[1], sc] for sc in range(SC)]
    turned = [pieces[(sc + 6) % SC] for sc in range(SC)]
    turned = [piece * sign if sc // 3 in (0, 3) else piece for sc, piece in enumerate(turned)]
    bra = jnp.concatenate(
        [jnp.concatenate(pieces, axis=1), jnp.concatenate(turned, axis=1)], axis=0
    )
    return lax.dot_general(
        bra, ket[...], (((1,), (1,)), ((), ())), preferred_element_type=jnp.float32
    )


def hop_kernel(
    counts,
    comm,
    start_ref,
    charge_ref,
    low_ref,
    link_ref,
    photon_ref,
    table_ref,
    out_ref,
    vall,
    vxy_a,
    vxy_b,
    perm,
    links,
    field,
    edge_out,
    edge_in,
    ket_s0,
    ket_s1,
    ket_p0,
    ket_p1,
    acc_s,
    acc_p,
    slots,
    local_sem,
    send_sem,
    recv_sem,
    sum_send,
    sum_recv,
):
    n_gz, n_ta = counts
    if comm:
        gz, ta = lax.axis_index("gz"), lax.axis_index("ta")
    else:
        gz, ta = jnp.int32(0), jnp.int32(0)

    def at(g, t):
        return {"gz": g, "ta": t}

    z_hi, x = gz // 4, gz % 4
    y, z_lo, core = ta // 4, (ta // 2) % 2, ta % 2
    z = z_hi * 2 + z_lo

    def group_a(index):
        return at(z_hi * 4 + index // 2, y * 4 + z_lo * 2 + index % 2)

    def group_b(index):
        return at((index // 2) * 4 + x, y * 4 + (index % 2) * 2 + core)

    def group_c(index):
        return at(gz, index * 4 + z_lo * 2 + core)

    stages = ((group_a, x * 2 + core), (group_b, z), (group_c, y))
    below_z = at((gz + n_gz - 1) % n_gz, ta)
    above_z = at((gz + 1) % n_gz, ta)
    below_t = at(gz, (ta + n_ta - 1) % n_ta)
    above_t = at(gz, (ta + 1) % n_ta)

    first_kind = z_lo == 0
    upper_up = jnp.logical_and(
        core == 1,
        jnp.logical_or(
            jnp.logical_and(x == 0, first_kind),
            jnp.logical_and(x == 3, jnp.logical_not(first_kind)),
        ),
    )
    lower_up = jnp.logical_and(
        core == 0,
        jnp.logical_or(
            jnp.logical_and(x == 0, jnp.logical_not(first_kind)),
            jnp.logical_and(x == 3, first_kind),
        ),
    )
    upper_down = jnp.logical_not(upper_up)
    lower_down = jnp.logical_not(lower_up)
    always = None

    barrier = pltpu.get_barrier_semaphore() if comm else None
    if comm:
        for device in (below_z, above_z, below_t, above_t):
            pl.semaphore_signal(barrier, inc=1, device_id=device, device_id_type=MESH)
        for group, index in stages:
            for step in range(1, 8):
                pl.semaphore_signal(
                    barrier, inc=1, device_id=group((index + step) % 8), device_id_type=MESH
                )

    own = [
        pltpu.make_async_copy(
            low_ref.at[t, zz], vall.at[t + 1, zz + 1], local_sem.at[t * 2 + zz]
        )
        for t in range(2)
        for zz in range(2)
    ]
    for copy in own:
        copy.start()

    def copy_to(src, dst, which, device):
        if comm:
            return pltpu.make_async_remote_copy(
                src_ref=src,
                dst_ref=dst,
                send_sem=send_sem.at[which],
                recv_sem=recv_sem.at[which],
                device_id=device,
                device_id_type=MESH,
            )
        return pltpu.make_async_copy(src, dst, recv_sem.at[which])

    down_z = (copy_to(low_ref.at[0, 0], vall.at[1, 3], 0, below_z), always, always)
    up_z = (copy_to(low_ref.at[1, 1], vall.at[2, 0], 1, above_z), always, always)
    down_t = [
        (copy_to(low_ref.at[0, zz], vall.at[3, zz + 1], 2 + zz, below_t), lower_down, upper_down)
        for zz in range(2)
    ]
    up_t = [
        (copy_to(low_ref.at[1, zz], vall.at[0, zz + 1], 4 + zz, above_t), upper_up, lower_up)
        for zz in range(2)
    ]
    edge_z = (copy_to(edge_out.at[0], edge_in.at[0], 6, above_z), always, always)
    edge_t = (
        copy_to(edge_out.at[pl.ds(1, 2)], edge_in.at[pl.ds(1, 2)], 7, above_t),
        upper_up,
        lower_up,
    )

    def guarded(flag, action):
        if flag is None:
            action()
        else:
            pl.when(flag)(action)

    def start(item):
        guarded(item[1], item[0].start)

    def arrive(item):
        guarded(item[2], item[0].wait_recv if comm else item[0].wait)

    if comm:
        pl.semaphore_wait(barrier, 25)
    for item in (down_z, up_z, *down_t, *up_t):
        start(item)

    def spread(t, _):
        turn = jnp.where(jnp.logical_and(ta == n_ta - 1, t == 1), -1.0, 1.0)
        for mu in range(4):
            photon = photon_ref[mu, t]
            scale = photon * turn if mu == 3 else photon
            for zz in range(2):
                field[t * 2 + zz, mu] = jnp.broadcast_to(photon[zz : zz + 1], (8, SITES))
            for entry in range(18):
                scaled = link_ref[mu, entry, t] * scale
                for zz in range(2):
                    links[t * 2 + zz, mu * 18 + entry] = jnp.broadcast_to(
                        scaled[zz : zz + 1], (8, SITES)
                    )
        return 0

    lax.fori_loop(0, 2, spread, 0)

    for number, (slot, mu) in enumerate(((3, 2), (2, 3), (3, 3))):
        rows = [links[slot, mu * 18 + entry, 0:1] for entry in range(18)]
        rows.append(field[slot, mu, 0:1])
        rows.append(jnp.zeros((EDGE - 19, SITES), jnp.float32))
        edge_out[number] = jnp.concatenate(rows, axis=0)
    start(edge_z)
    start(edge_t)

    row = lax.broadcasted_iota(jnp.int32, (SITES, SITES), 0)
    column = lax.broadcasted_iota(jnp.int32, (SITES, SITES), 1)
    along_x = (column + LY) % SITES
    along_y = (column - column % LY) + (column + 1) % LY
    perm[:, :SITES] = (row == along_x).astype(jnp.float32).astype(jnp.bfloat16)
    perm[:, SITES:] = (row == along_y).astype(jnp.float32).astype(jnp.bfloat16)

    acc_p[...] = jnp.zeros_like(acc_p)
    for copy in own:
        copy.wait()

    def shift(t, zz, vxy):
        vxy[...] = jnp.dot(
            vall[t + 1, zz + 1].reshape(ROWS, SITES),
            perm[...],
            preferred_element_type=jnp.float32,
        )

    shift(0, 0, vxy_a)

    def blocks(t, _):
        kets = (ket_s0, ket_s1)
        total = None
        pending = None
        for zz, vxy in ((0, vxy_a), (1, vxy_b)):
            if zz == 0:
                shift(t, 1, vxy_b)
            for lane in range(2):
                if pending is not None:
                    product = space_product(t, *pending, vall, kets[pending[1]])
                    total = product if total is None else total + product
                for half in range(2):
                    space_unit(t, zz, lane, half, vall, vxy, links, field, kets[lane])
                pending = (zz, lane)
            if zz == 0:
                shift(jnp.minimum(t + 1, 1), 0, vxy_a)
        acc_s[t] = total + space_product(t, *pending, vall, kets[pending[1]])
        return 0

    lax.fori_loop(0, 2, blocks, 0)

    def spread_edge(number, slot, mu):
        for entry in range(18):
            links[slot, mu * 18 + entry] = jnp.broadcast_to(
                edge_in[number, entry : entry + 1], (8, SITES)
            )
        field[slot, mu] = jnp.broadcast_to(edge_in[number, 18:19], (8, SITES))

    def pair(number, _):
        is_z = number == 3

        @pl.when(number == 1)
        def _():
            arrive(down_t[0])
            arrive(down_t[1])

        @pl.when(number == 2)
        def _():
            arrive(up_t[0])
            arrive(up_t[1])
            arrive(edge_t)

            @pl.when(lower_up)
            def _():
                spread_edge(1, 5, 3)
                spread_edge(2, 6, 3)

        @pl.when(is_z)
        def _():
            arrive(down_z)
            arrive(up_z)
            arrive(edge_z)
            spread_edge(0, 4, 2)

        active = jnp.logical_or(
            jnp.logical_or(number == 0, is_z),
            jnp.logical_or(
                jnp.logical_and(number == 1, upper_down), jnp.logical_and(number == 2, lower_up)
            ),
        )

        @pl.when(active)
        def _():
            mu = jnp.where(is_z, 2, 3)
            sign = jnp.where(is_z, -1.0, 1.0).astype(jnp.bfloat16)
            low_t = (number + 1) % 3
            spots = (
                (
                    (jnp.where(is_z, 1, low_t), jnp.where(is_z, 2, 1)),
                    (jnp.where(is_z, 1, low_t + 1), jnp.where(is_z, 3, 1)),
                    jnp.where(is_z, 1, jnp.where(number == 2, 5, number * 2)),
                ),
                (
                    (jnp.where(is_z, 2, low_t), jnp.where(is_z, 0, 2)),
                    (jnp.where(is_z, 2, low_t + 1), jnp.where(is_z, 1, 2)),
                    jnp.where(is_z, 4, jnp.where(number == 2, 6, number * 2 + 1)),
                ),
            )
            kets = (ket_p0, ket_p1)
            for which in range(2):
                low, up, slot = spots[which]
                for lane in range(2):
                    for half in range(2):
                        link_unit(up, slot, mu, lane, half, vall, links, field, kets[which])
                acc_p[number * 2 + which] = link_product(low, sign, vall, kets[which])

        return 0

    lax.fori_loop(0, 4, pair, 0)

    begin = start_ref[0]
    lattice_t = 2 * n_ta

    def inside(t):
        offset = (ta * 2 + t - begin + 2 * lattice_t) % lattice_t
        return jnp.where(offset < TW, 1.0, 0.0)

    before, first_in, last_in, after = (inside(t) for t in (-1, 0, 1, 2))

    def by_part(values, groups):
        rows = []
        for group in range(groups):
            for part in range(2):
                base = group * 32 + part * 8
                rows.append(
                    jnp.concatenate([values[base : base + 8], values[base + 16 : base + 24]], axis=0)
                )
        return jnp.concatenate(rows, axis=1)

    spaces = [by_part(acc_s[t], 1) for t in range(2)]
    times_in, times_up, times_low = (
        by_part(acc_p[2 * number] + acc_p[2 * number + 1], 2) for number in range(3)
    )
    z_links = [by_part(acc_p[6 + t], 2) for t in range(2)]
    space_in = first_in * spaces[0] + last_in * spaces[1]
    z_in = first_in * z_links[0] + last_in * z_links[1]
    raw = jnp.concatenate(
        [
            jnp.concatenate(
                [spaces[0] + spaces[1], times_in + times_up + times_low, z_links[0] + z_links[1]],
                axis=1,
            ),
            jnp.concatenate(
                [
                    space_in,
                    first_in * times_in + last_in * times_up + before * times_low,
                    z_in,
                ],
                axis=1,
            ),
            jnp.concatenate(
                [
                    space_in,
                    last_in * times_in + after * times_up + first_in * times_low,
                    z_in,
                ],
                axis=1,
            ),
        ],
        axis=0,
    )
    high, rest = split(raw)
    middle, low = split(raw - high.astype(jnp.float32))
    folded = jnp.dot(
        jnp.concatenate([high, middle, low], axis=0),
        table_ref[...],
        preferred_element_type=jnp.float32,
    )
    folded = folded[:48] + folded[48:96] + folded[96:]
    lane = lax.broadcasted_iota(jnp.int32, (1, 128), 1)
    windowed = jnp.where(lane < 64, folded[16:32], folded[32:])
    backward = jnp.transpose(jnp.concatenate([folded[:16], windowed], axis=0))[64:]
    pieces = [
        backward[group * 16 : group * 16 + 16, window * 16 : window * 16 + 16]
        for window in range(2)
        for group in range(4)
    ]
    value = jnp.concatenate([folded[:16, :64], windowed[:, :64]], axis=1)
    value = value + jnp.concatenate(pieces, axis=1)

    if comm:
        for number, (group, index) in enumerate(stages):
            slots[number, index] = value
            copies = []
            for hop in (4, 3, 5, 2, 6, 1, 7):
                copy = pltpu.make_async_remote_copy(
                    src_ref=slots.at[number, index],
                    dst_ref=slots.at[number, index],
                    send_sem=sum_send.at[number, hop],
                    recv_sem=sum_recv.at[number, index],
                    device_id=group((index + hop) % 8),
                    device_id_type=MESH,
                )
                copy.start()
                copies.append(copy)
            for hop in range(1, 8):
                peer = (index + hop) % 8
                pltpu.make_async_remote_copy(
                    src_ref=slots.at[number, peer],
                    dst_ref=slots.at[number, peer],
                    send_sem=sum_send.at[number, hop],
                    recv_sem=sum_recv.at[number, peer],
                    device_id=group(peer),
                    device_id_type=MESH,
                ).wait_recv()
            value = slots[number, 0]
            for other in range(1, 8):
                value = value + slots[number, other]
            for copy in copies:
                copy.wait_send()
        for item in (down_z, up_z, *down_t, *up_t, edge_z, edge_t):
            guarded(item[1], item[0].wait_send)

    charge = jnp.zeros((1, 128), jnp.float32)
    for mode in range(MODES):
        charge = jnp.where(lane % 16 == mode, charge_ref[mode].astype(jnp.float32), charge)
    charge = charge / 3.0
    volume = 24.0 * SITES * (2 * n_gz)
    scale = jnp.where(
        lane < 64, 1.0 / math.sqrt(volume * lattice_t), 1.0 / math.sqrt(volume * TW)
    )
    scale = scale * jnp.where(lane // 16 % 2 == 0, charge, charge * charge)
    out_ref[...] = value * scale


def insert_sums(counts, comm, low, links, photon, charges, start):
    vmem = pl.BlockSpec(memory_space=pltpu.VMEM)
    smem = pl.BlockSpec(memory_space=pltpu.SMEM)
    return pl.pallas_call(
        functools.partial(hop_kernel, counts, comm),
        out_shape=jax.ShapeDtypeStruct((MODES, 128), jnp.float32),
        in_specs=[smem, smem, pl.BlockSpec(memory_space=pl.ANY), vmem, vmem, vmem],
        out_specs=vmem,
        scratch_shapes=[
            pltpu.VMEM((4, 4, SC, 32, SITES), jnp.bfloat16),
            pltpu.VMEM((ROWS, 2 * SITES), jnp.float32),
            pltpu.VMEM((ROWS, 2 * SITES), jnp.float32),
            pltpu.VMEM((SITES, 2 * SITES), jnp.bfloat16),
            pltpu.VMEM((7, 72, 8, SITES), jnp.float32),
            pltpu.VMEM((7, 4, 8, SITES), jnp.float32),
            pltpu.VMEM((3, EDGE, SITES), jnp.float32),
            pltpu.VMEM((3, EDGE, SITES), jnp.float32),
            pltpu.VMEM((256, SC * 128), jnp.bfloat16),
            pltpu.VMEM((256, SC * 128), jnp.bfloat16),
            pltpu.VMEM((128, SC * SITES), jnp.bfloat16),
            pltpu.VMEM((128, SC * SITES), jnp.bfloat16),
            pltpu.VMEM((2, 32, 256), jnp.float32),
            pltpu.VMEM((8, 64, 128), jnp.float32),
            pltpu.VMEM((3, 8, MODES, 128), jnp.float32),
            pltpu.SemaphoreType.DMA((4,)),
            pltpu.SemaphoreType.DMA((8,)),
            pltpu.SemaphoreType.DMA((8,)),
            pltpu.SemaphoreType.DMA((3, 8)),
            pltpu.SemaphoreType.DMA((3, 8)),
        ],
        compiler_params=pltpu.CompilerParams(
            collective_id=0 if comm else None,
            has_side_effects=comm,
            vmem_limit_bytes=40 * 1024 * 1024,
        ),
    )(start, charges, low, links, photon, jnp.asarray(fold_table(), jnp.bfloat16))


def per_device(counts, comm, low_modes, gauge_links, photon, charges, window_start):
    low = low_modes.reshape(2, 8, 2, SC, 2, 2, SITES)
    low = low.transpose(4, 5, 3, 0, 2, 1, 6).reshape(2, 2, SC, 32, SITES)
    sums = insert_sums(counts, comm, low, gauge_links, photon, charges, window_start)
    sums = sums.reshape(MODES, 2, 2, 2, MODES)
    return tuple(
        jnp.transpose(sums[:, window, :, order], (1, 0, 2))
        for window in range(2)
        for order in range(2)
    )


def solution(mesh):
    counts = (mesh.shape["gz"], mesh.shape["ta"])
    return jax.shard_map(
        functools.partial(per_device, counts, True),
        mesh=mesh,
        in_specs=(
            P(None, None, None, None, "ta", "gz", None),
            P(None, None, "ta", "gz", None),
            P(None, "ta", "gz", None),
            P(),
            P(),
        ),
        out_specs=(P(), P(), P(), P()),
        check_vma=False,
    )
```

```python
import functools
import math

import jax
import jax.numpy as jnp
import numpy as np
from jax import lax
from jax.experimental import pallas as pl
from jax.experimental.pallas import tpu as pltpu
from jax.sharding import PartitionSpec as P

LY = 16
TW = 4
MODES = 16
SC = 12
SITES = 256
ROWS = SC * 32
EDGE = 24
MESH = pl.DeviceIdType.MESH

GAMMA = (
    ((3, 0, 1), (2, 0, 1), (1, 0, -1), (0, 0, -1)),
    ((3, -1, 0), (2, 1, 0), (1, 1, 0), (0, -1, 0)),
    ((2, 0, 1), (3, 0, -1), (0, 0, -1), (1, 0, 1)),
)


def fold_table():
    table = np.zeros((1536, 128), np.float32)

    def put(row, ket, order, plain, value):
        for side in range(2):
            factor = value * (0.5 if order == 0 else 0.25)
            if side == 0:
                factor = factor if plain else -factor
                factor = factor * (-1j if order == 0 else 1)
                parts = (factor.real, factor.imag)
            else:
                factor = np.conj(factor) * (1j if order == 0 else 1)
                parts = (factor.real, factor.imag)
            for part in range(2):
                table[row, side * 64 + part * 32 + order * 16 + ket] += parts[part]

    for bra in range(2):
        for half in range(2):
            for low in range(2):
                for part in range(2):
                    for mode in range(8):
                        ket = half * 8 + mode
                        value = (1, -1j)[bra] * (1, 1j)[part]
                        tail = low * 16 + part * 8 + mode
                        for kind in range(4):
                            row = bra * 256 + half * 128 + kind * 32 + tail
                            put(row, ket, kind // 2, kind % 2 == 0, value)
                        for order in range(2):
                            for turned in range(2):
                                row = (turned * 2 + bra) * 128 + half * 64 + order * 32 + tail
                                put(512 + row, ket, order, turned == 0, value)
                                phase = 1j if turned else 1
                                put(1024 + row, ket, order, turned == 0, value * phase)
    return table


def split(value):
    high = value.astype(jnp.bfloat16)
    low = (value - high.astype(jnp.float32)).astype(jnp.bfloat16)
    return high, low


def colour_row(rows, vectors):
    result = []
    for spin in range(4):
        total_re = None
        total_im = None
        for b in range(3):
            ur, ui = rows[b]
            value = vectors(spin * 3 + b)
            vr, vi = value[:8], value[8:]
            re = ur * vr - ui * vi
            im = ur * vi + ui * vr
            total_re = re if total_re is None else total_re + re
            total_im = im if total_im is None else total_im + im
        result.append((total_re, total_im))
    return result


def times(entry, pair):
    _, re, im = entry
    if re:
        return (re, pair[0]), (re, pair[1])
    return (-im, pair[1]), (im, pair[0])


def add_signed(total, sign, value):
    if total is None:
        return value if sign > 0 else -value
    return total + value if sign > 0 else total - value


def link_rows(links, slot, base, a, lanes):
    return [
        (links[slot, base + a * 3 + b, :, lanes], links[slot, base + 9 + a * 3 + b, :, lanes])
        for b in range(3)
    ]


def store_pair(ket, row, column, pair):
    high, low = split(jnp.concatenate(pair, axis=0))
    ket[row : row + 16, column : column + 128] = high
    ket[row + 16 : row + 32, column : column + 128] = low


def space_unit(t, zz, lane, half, vall, vxy, links, field, ket):
    lanes = slice(lane * 128, lane * 128 + 128)
    slot = t * 2 + zz

    def from_x(sc):
        return vxy[sc * 32 + half * 16 : sc * 32 + half * 16 + 16, lanes]

    def from_y(sc):
        row = sc * 32 + half * 16
        return vxy[row : row + 16, SITES + lane * 128 : SITES + lane * 128 + 128]

    def from_z(sc):
        rows = slice(half * 16, half * 16 + 16)
        return vall[t + 1, zz + 2, sc, rows, lanes].astype(jnp.float32)

    sources = (from_x, from_y, from_z) if zz == 0 else (from_x, from_y)
    for a in range(3):
        sums = [[[None, None] for _ in range(4)] for _ in range(4)]
        for mu, source in enumerate(sources):
            first = colour_row(link_rows(links, slot, mu * 18, a, lanes), source)
            photon = field[slot, mu, :, lanes]
            second = [(photon * re, photon * im) for re, im in first]
            for order, hopped in enumerate((first, second)):
                for spin in range(4):
                    plain = sums[order * 2][spin]
                    crossed = sums[order * 2 + 1][spin]
                    entry = GAMMA[mu][spin]
                    turned = times(entry, hopped[entry[0]])
                    for part in range(2):
                        plain[part] = add_signed(plain[part], 1, hopped[spin][part])
                        crossed[part] = add_signed(crossed[part], *turned[part])
        for kind in range(4):
            for spin in range(4):
                store_pair(ket, half * 128 + kind * 32, (spin * 3 + a) * 128, sums[kind][spin])


def space_product(t, zz, lane, chunk, vall, ket):
    lanes = slice(lane * 128, lane * 128 + 128)
    scs = range(chunk * 6, chunk * 6 + 6)
    bra = jnp.concatenate([vall[t + 1, zz + 1, sc, :, lanes] for sc in scs], axis=1)
    return [
        lax.dot_general(
            bra,
            ket[half * 128 : half * 128 + 128, chunk * 768 : chunk * 768 + 768],
            (((1,), (1,)), ((), ())),
            preferred_element_type=jnp.float32,
        )
        for half in range(2)
    ]


def link_unit(up, slot, mu, lane, half, vall, links, field, ket):
    lanes = slice(lane * 128, lane * 128 + 128)

    def source(sc):
        return vall[up[0], up[1], sc, half * 16 : half * 16 + 16, lanes].astype(jnp.float32)

    photon = field[slot, mu, :, lanes]
    for a in range(3):
        first = colour_row(link_rows(links, slot, mu * 18, a, lanes), source)
        for spin in range(4):
            re, im = first[spin]
            column = (spin * 3 + a) * SITES + lane * 128
            store_pair(ket, half * 64, column, (re, im))
            store_pair(ket, half * 64 + 32, column, (photon * re, photon * im))


def link_product(low, sign, chunk, vall, ket):
    scs = range(chunk * 3, chunk * 3 + 3)
    pieces = [vall[low[0], low[1], sc] for sc in scs]
    turned = [vall[low[0], low[1], (sc + 6) % SC] for sc in scs]
    if chunk in (0, 3):
        turned = [piece * sign for piece in turned]
    bra = jnp.concatenate(
        [jnp.concatenate(pieces, axis=1), jnp.concatenate(turned, axis=1)], axis=0
    )
    return [
        lax.dot_general(
            bra,
            ket[half * 64 : half * 64 + 64, chunk * 768 : chunk * 768 + 768],
            (((1,), (1,)), ((), ())),
            preferred_element_type=jnp.float32,
        )
        for half in range(2)
    ]


def plus(totals, parts):
    if totals is None:
        return parts
    return [total + part for total, part in zip(totals, parts)]


def hop_kernel(
    counts,
    comm,
    start_hbm,
    charge_hbm,
    low_ref,
    link_ref,
    photon_ref,
    table_ref,
    out_ref,
    start_ref,
    charge_ref,
    raw,
    raw_links,
    raw_photon,
    table,
    vall,
    vxy_a,
    vxy_b,
    perm,
    links,
    field,
    edge_out,
    edge_in,
    ket_s0,
    ket_s1,
    ket_p0,
    ket_p1,
    acc_s,
    acc_p,
    share,
    slots,
    whole,
    local_sem,
    send_sem,
    recv_sem,
    sum_send,
    sum_recv,
):
    n_gz, n_ta = counts
    own = [
        pltpu.make_async_copy(src, dst, local_sem.at[number])
        for number, (src, dst) in enumerate(
            (
                (low_ref, raw),
                (link_ref, raw_links),
                (photon_ref, raw_photon),
                (table_ref, table),
                (start_hbm, start_ref),
                (charge_hbm, charge_ref),
            )
        )
    ]
    for copy in own:
        copy.start()

    if comm:
        gz, ta = lax.axis_index("gz"), lax.axis_index("ta")
    else:
        gz, ta = jnp.int32(0), jnp.int32(0)

    def at(g, t):
        return {"gz": g, "ta": t}

    def wrapped(value, count):
        return jnp.where(value >= count, value - count, value)

    z_hi = lax.div(gz, 4)
    x = gz - z_hi * 4
    y = lax.div(ta, 4)
    inner = ta - y * 4
    z_lo = lax.div(inner, 2)
    core = inner - z_lo * 2
    z = z_hi * 2 + z_lo

    others_x, others_z, others_y = [], [], []
    for dx in (2, 1, 3):
        peer_x = wrapped(x + dx, 4)
        others_x.append((peer_x, at(z_hi * 4 + peer_x, ta)))
    for dz in (2, 1, 3, 0):
        peer_hi = wrapped(z_hi + dz, 4) if dz else z_hi
        for peer_lo in (z_lo, 1 - z_lo):
            if dz or peer_lo is not z_lo:
                others_z.append(
                    (peer_hi * 2 + peer_lo, at(peer_hi * 4 + x, ta + (peer_lo - z_lo) * 2))
                )
    for dy in (4, 3, 5, 2, 6, 1, 7):
        peer_y = wrapped(y + dy, 8)
        others_y.append((peer_y, at(gz, peer_y * 4 + inner)))
    stages = ((others_x, x), (others_z, z), (others_y, y))
    partner = at(gz, ta + 1 - 2 * core)
    is_first, is_second = core == 0, core == 1

    below_z = at(jnp.where(gz == 0, n_gz - 1, gz - 1), ta)
    above_z = at(wrapped(gz + 1, n_gz), ta)
    below_t = at(gz, jnp.where(ta == 0, n_ta - 1, ta - 1))
    above_t = at(gz, wrapped(ta + 1, n_ta))

    first_kind = z_lo == 0
    upper_up = jnp.logical_and(
        core == 1,
        jnp.logical_or(
            jnp.logical_and(x == 0, first_kind),
            jnp.logical_and(x == 3, jnp.logical_not(first_kind)),
        ),
    )
    lower_up = jnp.logical_and(
        core == 0,
        jnp.logical_or(
            jnp.logical_and(x == 0, jnp.logical_not(first_kind)),
            jnp.logical_and(x == 3, first_kind),
        ),
    )
    upper_down = jnp.logical_not(upper_up)
    lower_down = jnp.logical_not(lower_up)
    always = None

    barrier = pltpu.get_barrier_semaphore() if comm else None
    if comm:
        for device in (below_z, above_z, below_t, above_t, partner):
            pl.semaphore_signal(barrier, inc=1, device_id=device, device_id_type=MESH)

        @pl.when(is_second)
        def _():
            for group, _ in stages:
                for _, device in group:
                    pl.semaphore_signal(barrier, inc=1, device_id=device, device_id_type=MESH)

    def copy_to(src, dst, which, device):
        if comm:
            return pltpu.make_async_remote_copy(
                src_ref=src,
                dst_ref=dst,
                send_sem=send_sem.at[which],
                recv_sem=recv_sem.at[which],
                device_id=device,
                device_id_type=MESH,
            )
        return pltpu.make_async_copy(src, dst, recv_sem.at[which])

    down_z = (copy_to(vall.at[1, 1], vall.at[1, 3], 0, below_z), always, always)
    up_z = (copy_to(vall.at[2, 2], vall.at[2, 0], 1, above_z), always, always)
    down_t = [
        (copy_to(vall.at[1, zz + 1], vall.at[3, zz + 1], 2 + zz, below_t), lower_down, upper_down)
        for zz in range(2)
    ]
    up_t = [
        (copy_to(vall.at[2, zz + 1], vall.at[0, zz + 1], 4 + zz, above_t), upper_up, lower_up)
        for zz in range(2)
    ]
    edge_z = (copy_to(edge_out.at[0], edge_in.at[0], 6, above_z), always, always)
    edge_t = (
        copy_to(edge_out.at[pl.ds(1, 2)], edge_in.at[pl.ds(1, 2)], 7, above_t),
        upper_up,
        lower_up,
    )

    def guarded(flag, action):
        if flag is None:
            action()
        else:
            pl.when(flag)(action)

    def start(item):
        guarded(item[1], item[0].start)

    def arrive(item):
        guarded(item[2], item[0].wait_recv if comm else item[0].wait)

    row = lax.broadcasted_iota(jnp.int32, (SITES, SITES), 0)
    column = lax.broadcasted_iota(jnp.int32, (SITES, SITES), 1)
    along_x = (column + LY) % SITES
    along_y = (column - column % LY) + (column + 1) % LY
    perm[:, :SITES] = (row == along_x).astype(jnp.float32).astype(jnp.bfloat16)
    perm[:, SITES:] = (row == along_y).astype(jnp.float32).astype(jnp.bfloat16)
    acc_s[...] = jnp.zeros_like(acc_s)
    acc_p[...] = jnp.zeros_like(acc_p)
    ket_s1[...] = jnp.zeros_like(ket_s1)
    ket_p1[...] = jnp.zeros_like(ket_p1)

    def arrange(t):
        def one_spin(spin, _):
            for colour in range(3):
                parts = [
                    jnp.swapaxes(raw[:, part, spin, colour, t].astype(jnp.float32), 0, 1)
                    for part in range(2)
                ]
                for zz in range(2):
                    for half in range(2):
                        vall[
                            t + 1, zz + 1, spin * 3 + colour, half * 16 : half * 16 + 16, :
                        ] = jnp.concatenate(
                            [part[zz, half * 8 : half * 8 + 8] for part in parts], axis=0
                        ).astype(jnp.bfloat16)
            return 0

        lax.fori_loop(0, 4, one_spin, 0)

    own[0].wait()
    arrange(0)
    if comm:
        pl.semaphore_wait(barrier, jnp.where(is_second, 22, 5))
    for item in (down_z, *down_t):
        start(item)
    arrange(1)
    for item in (up_z, *up_t):
        start(item)

    own[1].wait()
    own[2].wait()

    def spread(t, _):
        turn = jnp.where(jnp.logical_and(ta == n_ta - 1, t == 1), -1.0, 1.0)
        for mu in range(4):
            photon = raw_photon[mu, t]
            scale = photon * turn if mu == 3 else photon
            for zz in range(2):
                field[t * 2 + zz, mu] = jnp.broadcast_to(photon[zz : zz + 1], (8, SITES))
            for entry in range(18):
                scaled = raw_links[mu, entry, t] * scale
                for zz in range(2):
                    links[t * 2 + zz, mu * 18 + entry] = jnp.broadcast_to(
                        scaled[zz : zz + 1], (8, SITES)
                    )
        return 0

    lax.fori_loop(0, 2, spread, 0)

    for number, (slot, mu) in enumerate(((3, 2), (2, 3), (3, 3))):
        rows = [links[slot, mu * 18 + entry, 0:1] for entry in range(18)]
        rows.append(field[slot, mu, 0:1])
        rows.append(jnp.zeros((EDGE - 19, SITES), jnp.float32))
        edge_out[number] = jnp.concatenate(rows, axis=0)
    start(edge_z)
    start(edge_t)

    def shift(t, zz, vxy):
        vxy[...] = jnp.dot(
            vall[t + 1, zz + 1].reshape(ROWS, SITES),
            perm[...],
            preferred_element_type=jnp.float32,
        )

    shift(0, 0, vxy_a)

    def blocks(t, _):
        kets = (ket_s0, ket_s1)
        before = jnp.maximum(t - 1, 0)
        pending = (before, 1, 1)
        for zz, vxy in ((0, vxy_a), (1, vxy_b)):
            for lane in range(2):
                if zz == 0 and lane == 0:
                    shift(t, 1, vxy_b)
                totals = None
                for half in range(2):
                    space_unit(t, zz, lane, half, vall, vxy, links, field, kets[lane])
                    totals = plus(totals, space_product(*pending, half, vall, kets[pending[2]]))
                for half in range(2):
                    acc_s[pending[0], half] += totals[half]
                pending = (t, zz, lane)
                if zz == 1 and lane == 0:
                    shift(jnp.minimum(t + 1, 1), 0, vxy_a)
        return 0

    lax.fori_loop(0, 2, blocks, 0)
    for chunk in range(2):
        for half, part in enumerate(space_product(1, 1, 1, chunk, vall, ket_s1)):
            acc_s[1, half] += part

    def spread_edge(number, slot, mu):
        for entry in range(18):
            links[slot, mu * 18 + entry] = jnp.broadcast_to(
                edge_in[number, entry : entry + 1], (8, SITES)
            )
        field[slot, mu] = jnp.broadcast_to(edge_in[number, 18:19], (8, SITES))

    z_first = jnp.where(x == 0, 0, 1)

    def place(number, which):
        z_t = z_first if which == 0 else 1 - z_first
        is_z = number == 3
        low_t = lax.rem(number + 1, 3)
        low = (jnp.where(is_z, z_t + 1, low_t), jnp.where(is_z, 2 - 2 * z_t, which + 1))
        up = (jnp.where(is_z, z_t + 1, low_t + 1), jnp.where(is_z, 3 - 2 * z_t, which + 1))
        slot = jnp.where(
            is_z, 1 + 3 * z_t, jnp.where(number == 2, 5, number * 2) + which
        )
        product = number * 2 + jnp.where(is_z, z_t, which)
        sign = jnp.where(is_z, -1.0, 1.0).astype(jnp.bfloat16)
        return low, up, slot, product, sign, z_t

    def product_of(number, which, ket, units=None):
        low, _, _, product, sign, _ = place(number, which)
        totals = None
        for chunk in range(4):
            if units is not None:
                units(chunk)
            totals = plus(totals, link_product(low, sign, chunk, vall, ket))
        for half in range(2):
            acc_p[product, half] = totals[half]

    def pair(number, previous):
        is_z = number == 3
        active = jnp.logical_or(
            jnp.logical_or(number == 0, is_z),
            jnp.logical_or(
                jnp.logical_and(number == 1, upper_down), jnp.logical_and(number == 2, lower_up)
            ),
        )

        @pl.when(active)
        def _():
            for which, ket in enumerate((ket_p0, ket_p1)):
                _, up, slot, _, _, z_t = place(number, which)

                @pl.when(number == 1)
                def _():
                    arrive(down_t[which])

                @pl.when(number == 2)
                def _():
                    arrive(up_t[which])
                    if which == 0:
                        arrive(edge_t)

                    @pl.when(lower_up)
                    def _():
                        spread_edge(1 + which, 5 + which, 3)

                @pl.when(jnp.logical_and(is_z, z_t == 0))
                def _():
                    arrive(down_z)

                @pl.when(jnp.logical_and(is_z, z_t == 1))
                def _():
                    arrive(up_z)
                    arrive(edge_z)
                    spread_edge(0, 4, 2)

                mu = jnp.where(is_z, 2, 3)

                def units(step, up=up, slot=slot, ket=ket):
                    link_unit(up, slot, mu, step // 2, step % 2, vall, links, field, ket)

                if which == 0:
                    product_of(previous, 1, ket_p1, units)
                else:
                    product_of(number, 0, ket_p0, units)

        return jnp.where(active, number, previous)

    lax.fori_loop(0, 4, pair, jnp.int32(0))
    product_of(jnp.int32(3), 1, ket_p1)

    own[4].wait()
    begin = start_ref[0]
    lattice_t = 2 * n_ta

    def inside(t):
        offset = (ta * 2 + t - begin + 2 * lattice_t) % lattice_t
        return jnp.where(offset < TW, 1.0, 0.0)

    before, first_in, last_in, after = (inside(t) for t in (-1, 0, 1, 2))

    def by_part(values, groups):
        rows = []
        for group in range(groups):
            for part in range(2):
                base = group * 32 + part * 8
                rows.append(
                    jnp.concatenate([values[base : base + 8], values[base + 16 : base + 24]], axis=0)
                )
        return jnp.concatenate(rows, axis=1)

    def both(acc, index):
        return jnp.concatenate([acc[index, 0], acc[index, 1]], axis=1)

    spaces = [by_part(both(acc_s, t), 1) for t in range(2)]
    times_in, times_up, times_low = (
        by_part(both(acc_p, 2 * number) + both(acc_p, 2 * number + 1), 2) for number in range(3)
    )
    z_links = [by_part(both(acc_p, 6 + t), 2) for t in range(2)]
    space_in = first_in * spaces[0] + last_in * spaces[1]
    z_in = first_in * z_links[0] + last_in * z_links[1]
    products = jnp.concatenate(
        [
            jnp.concatenate(
                [spaces[0] + spaces[1], times_in + times_up + times_low, z_links[0] + z_links[1]],
                axis=1,
            ),
            jnp.concatenate(
                [
                    space_in,
                    first_in * times_in + last_in * times_up + before * times_low,
                    z_in,
                ],
                axis=1,
            ),
            jnp.concatenate(
                [
                    space_in,
                    last_in * times_in + after * times_up + first_in * times_low,
                    z_in,
                ],
                axis=1,
            ),
        ],
        axis=0,
    )
    own[3].wait()
    own[5].wait()
    high, rest = split(products)
    middle, low = split(products - high.astype(jnp.float32))
    folded = jnp.dot(
        jnp.concatenate([high, middle, low], axis=0),
        table[...],
        preferred_element_type=jnp.float32,
    )
    folded = folded[:48] + folded[48:96] + folded[96:]
    lane = lax.broadcasted_iota(jnp.int32, (1, 128), 1)
    windowed = jnp.where(lane < 64, folded[16:32], folded[32:])
    backward = jnp.transpose(jnp.concatenate([folded[:16], windowed], axis=0))[64:]
    pieces = [
        backward[group * 16 : group * 16 + 16, window * 16 : window * 16 + 16]
        for window in range(2)
        for group in range(4)
    ]
    value = jnp.concatenate([folded[:16, :64], windowed[:, :64]], axis=1)
    value = value + jnp.concatenate(pieces, axis=1)

    if comm:

        def to_partner(ref, number):
            return pltpu.make_async_remote_copy(
                src_ref=ref,
                dst_ref=ref,
                send_sem=sum_send.at[number, 7],
                recv_sem=sum_recv.at[3, number],
                device_id=partner,
                device_id_type=MESH,
            )

        hand_over = to_partner(share, 0)
        hand_back = to_partner(whole, 1)

        @pl.when(is_first)
        def _():
            share[...] = value
            hand_over.start()
            hand_back.wait_recv()
            hand_over.wait_send()

        @pl.when(is_second)
        def _():
            hand_over.wait_recv()
            total = value + share[...]
            started = []
            for number, (others, index) in enumerate(stages):
                slots[number, index] = total
                for step, (_, device) in enumerate(others):
                    copy = pltpu.make_async_remote_copy(
                        src_ref=slots.at[number, index],
                        dst_ref=slots.at[number, index],
                        send_sem=sum_send.at[number, step],
                        recv_sem=sum_recv.at[number, index],
                        device_id=device,
                        device_id_type=MESH,
                    )
                    copy.start()
                    started.append(copy)
                for step, (peer, device) in enumerate(others):
                    pltpu.make_async_remote_copy(
                        src_ref=slots.at[number, peer],
                        dst_ref=slots.at[number, peer],
                        send_sem=sum_send.at[number, step],
                        recv_sem=sum_recv.at[number, peer],
                        device_id=device,
                        device_id_type=MESH,
                    ).wait_recv()
                total = slots[number, 0]
                for other in range(1, len(others) + 1):
                    total = total + slots[number, other]
            whole[...] = total
            hand_back.start()
            for copy in started:
                copy.wait_send()
            hand_back.wait_send()

        value = whole[...]
        for item in (down_z, up_z, *down_t, *up_t, edge_z, edge_t):
            guarded(item[1], item[0].wait_send)

    charge = jnp.zeros((1, 128), jnp.float32)
    for mode in range(MODES):
        charge = jnp.where(lane % 16 == mode, charge_ref[mode].astype(jnp.float32), charge)
    charge = charge / 3.0
    volume = 24.0 * SITES * (2 * n_gz)
    scale = jnp.where(
        lane < 64, 1.0 / math.sqrt(volume * lattice_t), 1.0 / math.sqrt(volume * TW)
    )
    scale = scale * jnp.where(lane // 16 % 2 == 0, charge, charge * charge)
    out_ref[...] = value * scale


def insert_sums(counts, comm, low, links, photon, charges, start):
    vmem = pl.BlockSpec(memory_space=pltpu.VMEM)
    return pl.pallas_call(
        functools.partial(hop_kernel, counts, comm),
        out_shape=jax.ShapeDtypeStruct((MODES, 128), jnp.float32),
        in_specs=[pl.BlockSpec(memory_space=pl.ANY)] * 6,
        out_specs=vmem,
        scratch_shapes=[
            pltpu.SMEM(start.shape, start.dtype),
            pltpu.SMEM(charges.shape, charges.dtype),
            pltpu.VMEM(low.shape, low.dtype),
            pltpu.VMEM(links.shape, links.dtype),
            pltpu.VMEM(photon.shape, photon.dtype),
            pltpu.VMEM((1536, 128), jnp.bfloat16),
            pltpu.VMEM((4, 4, SC, 32, SITES), jnp.bfloat16),
            pltpu.VMEM((ROWS, 2 * SITES), jnp.float32),
            pltpu.VMEM((ROWS, 2 * SITES), jnp.float32),
            pltpu.VMEM((SITES, 2 * SITES), jnp.bfloat16),
            pltpu.VMEM((7, 72, 8, SITES), jnp.float32),
            pltpu.VMEM((7, 4, 8, SITES), jnp.float32),
            pltpu.VMEM((3, EDGE, SITES), jnp.float32),
            pltpu.VMEM((3, EDGE, SITES), jnp.float32),
            pltpu.VMEM((256, SC * 128), jnp.bfloat16),
            pltpu.VMEM((256, SC * 128), jnp.bfloat16),
            pltpu.VMEM((128, SC * SITES), jnp.bfloat16),
            pltpu.VMEM((128, SC * SITES), jnp.bfloat16),
            pltpu.VMEM((2, 2, 32, 128), jnp.float32),
            pltpu.VMEM((8, 2, 64, 64), jnp.float32),
            pltpu.VMEM((MODES, 128), jnp.float32),
            pltpu.VMEM((3, 8, MODES, 128), jnp.float32),
            pltpu.VMEM((MODES, 128), jnp.float32),
            pltpu.SemaphoreType.DMA((6,)),
            pltpu.SemaphoreType.DMA((8,)),
            pltpu.SemaphoreType.DMA((8,)),
            pltpu.SemaphoreType.DMA((3, 8)),
            pltpu.SemaphoreType.DMA((4, 8)),
        ],
        compiler_params=pltpu.CompilerParams(
            collective_id=0 if comm else None,
            has_side_effects=comm,
            vmem_limit_bytes=60 * 1024 * 1024,
        ),
    )(start, charges, low, links, photon, jnp.asarray(fold_table(), jnp.bfloat16))


def per_device(counts, comm, low_modes, gauge_links, photon, charges, window_start):
    sums = insert_sums(counts, comm, low_modes, gauge_links, photon, charges, window_start)
    sums = sums.reshape(MODES, 2, 2, 2, MODES)
    return tuple(
        jnp.transpose(sums[:, window, :, order], (1, 0, 2))
        for window in range(2)
        for order in range(2)
    )


def solution(mesh):
    counts = (mesh.shape["gz"], mesh.shape["ta"])
    return jax.shard_map(
        functools.partial(per_device, counts, True),
        mesh=mesh,
        in_specs=(
            P(None, None, None, None, "ta", "gz", None),
            P(None, None, "ta", "gz", None),
            P(None, "ta", "gz", None),
            P(),
            P(),
        ),
        out_specs=(P(), P(), P(), P()),
        check_vma=False,
    )
```

```python
import functools
import math

import jax
import jax.numpy as jnp
import numpy as np
from jax import lax
from jax.experimental import pallas as pl
from jax.experimental.pallas import tpu as pltpu
from jax.sharding import PartitionSpec as P

LY = 16
TW = 4
MODES = 16
SC = 12
SITES = 256
ROWS = SC * 32
EDGE = 24
MESH = pl.DeviceIdType.MESH

GAMMA = (
    ((3, 0, 1), (2, 0, 1), (1, 0, -1), (0, 0, -1)),
    ((3, -1, 0), (2, 1, 0), (1, 1, 0), (0, -1, 0)),
    ((2, 0, 1), (3, 0, -1), (0, 0, -1), (1, 0, 1)),
)


def fold_table():
    table = np.zeros((1536, 128), np.float32)

    def put(row, ket, order, plain, value):
        for side in range(2):
            factor = value * (0.5 if order == 0 else 0.25)
            if side == 0:
                factor = factor if plain else -factor
                factor = factor * (-1j if order == 0 else 1)
                parts = (factor.real, factor.imag)
            else:
                factor = np.conj(factor) * (1j if order == 0 else 1)
                parts = (factor.real, factor.imag)
            for part in range(2):
                table[row, side * 64 + part * 32 + order * 16 + ket] += parts[part]

    for bra in range(2):
        for half in range(2):
            for low in range(2):
                for part in range(2):
                    for mode in range(8):
                        ket = half * 8 + mode
                        value = (1, -1j)[bra] * (1, 1j)[part]
                        tail = low * 16 + part * 8 + mode
                        for kind in range(4):
                            row = bra * 256 + half * 128 + kind * 32 + tail
                            put(row, ket, kind // 2, kind % 2 == 0, value)
                        for order in range(2):
                            for turned in range(2):
                                row = (turned * 2 + bra) * 128 + half * 64 + order * 32 + tail
                                put(512 + row, ket, order, turned == 0, value)
                                phase = 1j if turned else 1
                                put(1024 + row, ket, order, turned == 0, value * phase)
    return table


def split(value):
    high = value.astype(jnp.bfloat16)
    low = (value - high.astype(jnp.float32)).astype(jnp.bfloat16)
    return high, low


def colour_row(rows, vectors):
    result = []
    for spin in range(4):
        total_re = None
        total_im = None
        for b in range(3):
            ur, ui = rows[b]
            value = vectors(spin * 3 + b)
            vr, vi = value[:8], value[8:]
            re = ur * vr - ui * vi
            im = ur * vi + ui * vr
            total_re = re if total_re is None else total_re + re
            total_im = im if total_im is None else total_im + im
        result.append((total_re, total_im))
    return result


def times(entry, pair):
    _, re, im = entry
    if re:
        return (re, pair[0]), (re, pair[1])
    return (-im, pair[1]), (im, pair[0])


def add_signed(total, sign, value):
    if total is None:
        return value if sign > 0 else -value
    return total + value if sign > 0 else total - value


def link_rows(links, slot, base, a, lanes):
    return [
        (links[slot, base + a * 3 + b, :, lanes], links[slot, base + 9 + a * 3 + b, :, lanes])
        for b in range(3)
    ]


def store_pair(ket, row, column, pair):
    high, low = split(jnp.concatenate(pair, axis=0))
    ket[row : row + 16, column : column + 128] = high
    ket[row + 16 : row + 32, column : column + 128] = low


def space_unit(t, zz, lane, half, vall, vxy, links, field, ket):
    lanes = slice(lane * 128, lane * 128 + 128)
    slot = t * 2 + zz

    def from_x(sc):
        return vxy[sc * 32 + half * 16 : sc * 32 + half * 16 + 16, lanes]

    def from_y(sc):
        row = sc * 32 + half * 16
        return vxy[row : row + 16, SITES + lane * 128 : SITES + lane * 128 + 128]

    def from_z(sc):
        rows = slice(half * 16, half * 16 + 16)
        return vall[t + 1, zz + 2, sc, rows, lanes].astype(jnp.float32)

    sources = (from_x, from_y, from_z) if zz == 0 else (from_x, from_y)
    for a in range(3):
        hops = [
            colour_row(link_rows(links, slot, mu * 18, a, lanes), source)
            for mu, source in enumerate(sources)
        ]
        for order in range(2):
            if order == 1:
                for mu in range(len(hops)):
                    photon = field[slot, mu, :, lanes]
                    hops[mu] = [(photon * re, photon * im) for re, im in hops[mu]]
            for spin in range(4):
                plain = [None, None]
                crossed = [None, None]
                for mu, hopped in enumerate(hops):
                    entry = GAMMA[mu][spin]
                    turned = times(entry, hopped[entry[0]])
                    for part in range(2):
                        plain[part] = add_signed(plain[part], 1, hopped[spin][part])
                        crossed[part] = add_signed(crossed[part], *turned[part])
                column = (spin * 3 + a) * 128
                store_pair(ket, half * 128 + order * 64, column, plain)
                store_pair(ket, half * 128 + order * 64 + 32, column, crossed)


def space_product(t, zz, lane, chunk, vall, ket):
    lanes = slice(lane * 128, lane * 128 + 128)
    scs = range(chunk * 6, chunk * 6 + 6)
    bra = jnp.concatenate([vall[t + 1, zz + 1, sc, :, lanes] for sc in scs], axis=1)
    return [
        lax.dot_general(
            bra,
            ket[half * 128 : half * 128 + 128, chunk * 768 : chunk * 768 + 768],
            (((1,), (1,)), ((), ())),
            preferred_element_type=jnp.float32,
        )
        for half in range(2)
    ]


def link_unit(up, slot, mu, lane, half, vall, links, field, ket):
    lanes = slice(lane * 128, lane * 128 + 128)

    def source(sc):
        return vall[up[0], up[1], sc, half * 16 : half * 16 + 16, lanes].astype(jnp.float32)

    photon = field[slot, mu, :, lanes]
    for a in range(3):
        first = colour_row(link_rows(links, slot, mu * 18, a, lanes), source)
        for spin in range(4):
            re, im = first[spin]
            column = (spin * 3 + a) * SITES + lane * 128
            store_pair(ket, half * 64, column, (re, im))
            store_pair(ket, half * 64 + 32, column, (photon * re, photon * im))


def link_product(low, sign, chunk, vall, ket):
    scs = range(chunk * 3, chunk * 3 + 3)
    pieces = [vall[low[0], low[1], sc] for sc in scs]
    turned = [vall[low[0], low[1], (sc + 6) % SC] for sc in scs]
    if chunk in (0, 3):
        turned = [piece * sign for piece in turned]
    bra = jnp.concatenate(
        [jnp.concatenate(pieces, axis=1), jnp.concatenate(turned, axis=1)], axis=0
    )
    return [
        lax.dot_general(
            bra,
            ket[half * 64 : half * 64 + 64, chunk * 768 : chunk * 768 + 768],
            (((1,), (1,)), ((), ())),
            preferred_element_type=jnp.float32,
        )
        for half in range(2)
    ]


def plus(totals, parts):
    if totals is None:
        return parts
    return [total + part for total, part in zip(totals, parts)]


def hop_kernel(
    counts,
    comm,
    start_hbm,
    charge_hbm,
    low_ref,
    link_ref,
    photon_ref,
    table_ref,
    out_ref,
    start_ref,
    charge_ref,
    raw,
    raw_links,
    raw_photon,
    table,
    vall,
    vxy_a,
    vxy_b,
    perm,
    links,
    field,
    edge_out,
    edge_in,
    ket_s0,
    ket_s1,
    ket_p0,
    ket_p1,
    acc_s,
    acc_p,
    share,
    slots,
    whole,
    local_sem,
    send_sem,
    recv_sem,
    sum_send,
    sum_recv,
):
    n_gz, n_ta = counts
    own = [
        pltpu.make_async_copy(src, dst, local_sem.at[number])
        for number, (src, dst) in enumerate(
            (
                (low_ref, raw),
                (link_ref, raw_links),
                (photon_ref, raw_photon),
                (table_ref, table),
                (start_hbm, start_ref),
                (charge_hbm, charge_ref),
            )
        )
    ]
    for copy in own:
        copy.start()

    if comm:
        gz, ta = lax.axis_index("gz"), lax.axis_index("ta")
    else:
        gz, ta = jnp.int32(0), jnp.int32(0)

    def at(g, t):
        return {"gz": g, "ta": t}

    def wrapped(value, count):
        return jnp.where(value >= count, value - count, value)

    z_hi = lax.div(gz, 4)
    x = gz - z_hi * 4
    y = lax.div(ta, 4)
    inner = ta - y * 4
    z_lo = lax.div(inner, 2)
    core = inner - z_lo * 2
    z = z_hi * 2 + z_lo

    others_x, others_z, others_y = [], [], []
    for dx in (2, 1, 3):
        peer_x = wrapped(x + dx, 4)
        others_x.append((peer_x, at(z_hi * 4 + peer_x, ta)))
    for dz in (2, 1, 3, 0):
        peer_hi = wrapped(z_hi + dz, 4) if dz else z_hi
        for peer_lo in (z_lo, 1 - z_lo):
            if dz or peer_lo is not z_lo:
                others_z.append(
                    (peer_hi * 2 + peer_lo, at(peer_hi * 4 + x, ta + (peer_lo - z_lo) * 2))
                )
    for dy in (4, 3, 5, 2, 6, 1, 7):
        peer_y = wrapped(y + dy, 8)
        others_y.append((peer_y, at(gz, peer_y * 4 + inner)))
    stages = ((others_x, x), (others_z, z), (others_y, y))
    crossed = ta + 1 - 2 * core
    along_row = [(x, at(gz, crossed))]
    along_row += [
        (wrapped(x + dx, 4), at(z_hi * 4 + wrapped(x + dx, 4), crossed)) for dx in (2, 1, 3)
    ]
    along_column = [(y, at(gz, crossed))]
    along_column += [
        (wrapped(y + dy, 8), at(gz, wrapped(y + dy, 8) * 4 + crossed - y * 4))
        for dy in (4, 3, 5, 2, 6, 1, 7)
    ]
    is_first, is_second = core == 0, core == 1

    below_z = at(jnp.where(gz == 0, n_gz - 1, gz - 1), ta)
    above_z = at(wrapped(gz + 1, n_gz), ta)
    below_t = at(gz, jnp.where(ta == 0, n_ta - 1, ta - 1))
    above_t = at(gz, wrapped(ta + 1, n_ta))

    first_kind = z_lo == 0
    upper_up = jnp.logical_and(
        core == 1,
        jnp.logical_or(
            jnp.logical_and(x == 0, first_kind),
            jnp.logical_and(x == 3, jnp.logical_not(first_kind)),
        ),
    )
    lower_up = jnp.logical_and(
        core == 0,
        jnp.logical_or(
            jnp.logical_and(x == 0, jnp.logical_not(first_kind)),
            jnp.logical_and(x == 3, first_kind),
        ),
    )
    upper_down = jnp.logical_not(upper_up)
    lower_down = jnp.logical_not(lower_up)
    always = None

    barrier = pltpu.get_barrier_semaphore() if comm else None
    if comm:
        greeted = [below_z, above_z, below_t, above_t]
        greeted += [device for _, device in along_row + along_column]
        for device in greeted:
            pl.semaphore_signal(barrier, inc=1, device_id=device, device_id_type=MESH)

        @pl.when(is_second)
        def _():
            for group, _ in stages:
                for _, device in group:
                    pl.semaphore_signal(barrier, inc=1, device_id=device, device_id_type=MESH)

    def copy_to(src, dst, which, device):
        if comm:
            return pltpu.make_async_remote_copy(
                src_ref=src,
                dst_ref=dst,
                send_sem=send_sem.at[which],
                recv_sem=recv_sem.at[which],
                device_id=device,
                device_id_type=MESH,
            )
        return pltpu.make_async_copy(src, dst, recv_sem.at[which])

    down_z = (copy_to(vall.at[1, 1], vall.at[1, 3], 0, below_z), always, always)
    up_z = (copy_to(vall.at[2, 2], vall.at[2, 0], 1, above_z), always, always)
    down_t = [
        (copy_to(vall.at[1, zz + 1], vall.at[3, zz + 1], 2 + zz, below_t), lower_down, upper_down)
        for zz in range(2)
    ]
    up_t = [
        (copy_to(vall.at[2, zz + 1], vall.at[0, zz + 1], 4 + zz, above_t), upper_up, lower_up)
        for zz in range(2)
    ]
    edge_z = (copy_to(edge_out.at[0], edge_in.at[0], 6, above_z), always, always)
    edge_t = (
        copy_to(edge_out.at[pl.ds(1, 2)], edge_in.at[pl.ds(1, 2)], 7, above_t),
        upper_up,
        lower_up,
    )

    def guarded(flag, action):
        if flag is None:
            action()
        else:
            pl.when(flag)(action)

    def start(item):
        guarded(item[1], item[0].start)

    def arrive(item):
        guarded(item[2], item[0].wait_recv if comm else item[0].wait)

    row = lax.broadcasted_iota(jnp.int32, (SITES, SITES), 0)
    column = lax.broadcasted_iota(jnp.int32, (SITES, SITES), 1)
    along_x = (column + LY) % SITES
    along_y = (column - column % LY) + (column + 1) % LY
    perm[:, :SITES] = (row == along_x).astype(jnp.float32).astype(jnp.bfloat16)
    perm[:, SITES:] = (row == along_y).astype(jnp.float32).astype(jnp.bfloat16)
    acc_s[...] = jnp.zeros_like(acc_s)
    acc_p[...] = jnp.zeros_like(acc_p)
    ket_s1[...] = jnp.zeros_like(ket_s1)
    ket_p1[...] = jnp.zeros_like(ket_p1)

    def arrange(t):
        def one_spin(spin, _):
            for colour in range(3):
                parts = [
                    jnp.swapaxes(raw[:, part, spin, colour, t].astype(jnp.float32), 0, 1)
                    for part in range(2)
                ]
                for zz in range(2):
                    for half in range(2):
                        vall[
                            t + 1, zz + 1, spin * 3 + colour, half * 16 : half * 16 + 16, :
                        ] = jnp.concatenate(
                            [part[zz, half * 8 : half * 8 + 8] for part in parts], axis=0
                        ).astype(jnp.bfloat16)
            return 0

        lax.fori_loop(0, 4, one_spin, 0)

    own[0].wait()
    arrange(0)
    if comm:
        pl.semaphore_wait(barrier, jnp.where(is_second, 33, 16))
    for item in (down_z, *down_t):
        start(item)
    arrange(1)
    for item in (up_z, *up_t):
        start(item)

    own[1].wait()
    own[2].wait()

    def spread(t, _):
        turn = jnp.where(jnp.logical_and(ta == n_ta - 1, t == 1), -1.0, 1.0)
        for mu in range(4):
            photon = raw_photon[mu, t]
            scale = photon * turn if mu == 3 else photon
            for zz in range(2):
                field[t * 2 + zz, mu] = jnp.broadcast_to(photon[zz : zz + 1], (8, SITES))
            for entry in range(18):
                scaled = raw_links[mu, entry, t] * scale
                for zz in range(2):
                    links[t * 2 + zz, mu * 18 + entry] = jnp.broadcast_to(
                        scaled[zz : zz + 1], (8, SITES)
                    )
        return 0

    lax.fori_loop(0, 2, spread, 0)

    for number, (slot, mu) in enumerate(((3, 2), (2, 3), (3, 3))):
        rows = [links[slot, mu * 18 + entry, 0:1] for entry in range(18)]
        rows.append(field[slot, mu, 0:1])
        rows.append(jnp.zeros((EDGE - 19, SITES), jnp.float32))
        edge_out[number] = jnp.concatenate(rows, axis=0)
    start(edge_z)
    start(edge_t)

    def shift(t, zz, vxy):
        vxy[...] = jnp.dot(
            vall[t + 1, zz + 1].reshape(ROWS, SITES),
            perm[...],
            preferred_element_type=jnp.float32,
        )

    def shift_half(t, zz, vxy, part):
        vxy[part * 192 : part * 192 + 192, :] = jnp.dot(
            vall[t + 1, zz + 1, part * 6 : part * 6 + 6].reshape(192, SITES),
            perm[...],
            preferred_element_type=jnp.float32,
        )

    shift(0, 0, vxy_a)

    def blocks(t, _):
        kets = (ket_s0, ket_s1)
        pending = (jnp.maximum(t - 1, 0), 1, 1)
        for zz, vxy in ((0, vxy_a), (1, vxy_b)):
            for lane in range(2):

                @pl.when(core >= 0)
                def _(zz=zz, vxy=vxy, lane=lane, pending=pending):
                    totals = None
                    for half in range(2):
                        space_unit(t, zz, lane, half, vall, vxy, links, field, kets[lane])
                        totals = plus(totals, space_product(*pending, half, vall, kets[pending[2]]))
                    for half in range(2):
                        acc_s[pending[0], half] += totals[half]
                    if zz == 0:
                        shift_half(t, 1, vxy_b, lane)
                    else:
                        shift_half(jnp.minimum(t + 1, 1), 0, vxy_a, lane)

                pending = (t, zz, lane)
        return 0

    lax.fori_loop(0, 2, blocks, 0)
    for chunk in range(2):
        for half, part in enumerate(space_product(1, 1, 1, chunk, vall, ket_s1)):
            acc_s[1, half] += part

    def spread_edge(number, slot, mu):
        for entry in range(18):
            links[slot, mu * 18 + entry] = jnp.broadcast_to(
                edge_in[number, entry : entry + 1], (8, SITES)
            )
        field[slot, mu] = jnp.broadcast_to(edge_in[number, 18:19], (8, SITES))

    z_first = jnp.where(x == 0, 0, 1)

    def place(number, which):
        z_t = z_first if which == 0 else 1 - z_first
        is_z = number == 3
        low_t = lax.rem(number + 1, 3)
        low = (jnp.where(is_z, z_t + 1, low_t), jnp.where(is_z, 2 - 2 * z_t, which + 1))
        up = (jnp.where(is_z, z_t + 1, low_t + 1), jnp.where(is_z, 3 - 2 * z_t, which + 1))
        slot = jnp.where(
            is_z, 1 + 3 * z_t, jnp.where(number == 2, 5, number * 2) + which
        )
        product = number * 2 + jnp.where(is_z, z_t, which)
        sign = jnp.where(is_z, -1.0, 1.0).astype(jnp.bfloat16)
        return low, up, slot, product, sign, z_t

    def product_of(number, which, ket, units=None):
        low, _, _, product, sign, _ = place(number, which)
        totals = None
        for chunk in range(4):
            if units is not None:
                units(chunk)
            totals = plus(totals, link_product(low, sign, chunk, vall, ket))
        for half in range(2):
            acc_p[product, half] = totals[half]

    def pair(number, previous):
        is_z = number == 3
        active = jnp.logical_or(
            jnp.logical_or(number == 0, is_z),
            jnp.logical_or(
                jnp.logical_and(number == 1, upper_down), jnp.logical_and(number == 2, lower_up)
            ),
        )

        @pl.when(active)
        def _():
            for which, ket in enumerate((ket_p0, ket_p1)):
                _, up, slot, _, _, z_t = place(number, which)

                @pl.when(number == 1)
                def _():
                    arrive(down_t[which])

                @pl.when(number == 2)
                def _():
                    arrive(up_t[which])
                    if which == 0:
                        arrive(edge_t)

                    @pl.when(lower_up)
                    def _():
                        spread_edge(1 + which, 5 + which, 3)

                @pl.when(jnp.logical_and(is_z, z_t == 0))
                def _():
                    arrive(down_z)

                @pl.when(jnp.logical_and(is_z, z_t == 1))
                def _():
                    arrive(up_z)
                    arrive(edge_z)
                    spread_edge(0, 4, 2)

                mu = jnp.where(is_z, 2, 3)

                def units(step, up=up, slot=slot, ket=ket):
                    link_unit(up, slot, mu, step // 2, step % 2, vall, links, field, ket)

                if which == 0:
                    product_of(previous, 1, ket_p1, units)
                else:
                    product_of(number, 0, ket_p0, units)

        return jnp.where(active, number, previous)

    lax.fori_loop(0, 4, pair, jnp.int32(0))
    product_of(jnp.int32(3), 1, ket_p1)

    own[4].wait()
    begin = start_ref[0]
    lattice_t = 2 * n_ta

    def inside(t):
        offset = (ta * 2 + t - begin + 2 * lattice_t) % lattice_t
        return jnp.where(offset < TW, 1.0, 0.0)

    before, first_in, last_in, after = (inside(t) for t in (-1, 0, 1, 2))

    def by_part(values, groups):
        rows = []
        for group in range(groups):
            for part in range(2):
                base = group * 32 + part * 8
                rows.append(
                    jnp.concatenate([values[base : base + 8], values[base + 16 : base + 24]], axis=0)
                )
        return jnp.concatenate(rows, axis=1)

    def both(acc, index):
        return jnp.concatenate([acc[index, 0], acc[index, 1]], axis=1)

    spaces = [by_part(both(acc_s, t), 1) for t in range(2)]
    times_in, times_up, times_low = (
        by_part(both(acc_p, 2 * number) + both(acc_p, 2 * number + 1), 2) for number in range(3)
    )
    z_links = [by_part(both(acc_p, 6 + t), 2) for t in range(2)]
    space_in = first_in * spaces[0] + last_in * spaces[1]
    z_in = first_in * z_links[0] + last_in * z_links[1]
    products = jnp.concatenate(
        [
            jnp.concatenate(
                [spaces[0] + spaces[1], times_in + times_up + times_low, z_links[0] + z_links[1]],
                axis=1,
            ),
            jnp.concatenate(
                [
                    space_in,
                    first_in * times_in + last_in * times_up + before * times_low,
                    z_in,
                ],
                axis=1,
            ),
            jnp.concatenate(
                [
                    space_in,
                    last_in * times_in + after * times_up + first_in * times_low,
                    z_in,
                ],
                axis=1,
            ),
        ],
        axis=0,
    )
    own[3].wait()
    own[5].wait()
    high, rest = split(products)
    middle, low = split(products - high.astype(jnp.float32))
    folded = jnp.dot(
        jnp.concatenate([high, middle, low], axis=0),
        table[...],
        preferred_element_type=jnp.float32,
    )
    folded = folded[:48] + folded[48:96] + folded[96:]
    lane = lax.broadcasted_iota(jnp.int32, (1, 128), 1)
    windowed = jnp.where(lane < 64, folded[16:32], folded[32:])
    backward = jnp.transpose(jnp.concatenate([folded[:16], windowed], axis=0))[64:]
    pieces = [
        backward[group * 16 : group * 16 + 16, window * 16 : window * 16 + 16]
        for window in range(2)
        for group in range(4)
    ]
    value = jnp.concatenate([folded[:16, :64], windowed[:, :64]], axis=1)
    value = value + jnp.concatenate(pieces, axis=1)

    if comm:

        def message(src, number, slot, sent, device):
            return pltpu.make_async_remote_copy(
                src_ref=src,
                dst_ref=slots.at[number, slot],
                send_sem=sum_send.at[sent],
                recv_sem=sum_recv.at[number, slot],
                device_id=device,
                device_id_type=MESH,
            )

        def gather(number, found, last):
            for slot, device in found:
                message(slots.at[number, slot], number, slot, 0, device).wait_recv()
            total = slots[number, 0]
            for other in range(1, last):
                total = total + slots[number, other]
            return total

        @pl.when(is_first)
        def _():
            share[...] = value
            started = [
                message(share, 0, 4 + x, step, device)
                for step, (_, device) in enumerate(along_row)
            ]
            for copy in started:
                copy.start()
            whole[...] = gather(2, along_column, 8)
            for copy in started:
                copy.wait_send()

        @pl.when(is_second)
        def _():
            total = value
            started = []
            for number, (others, index) in enumerate(stages):
                slots[number, index] = total
                targets = [(index, device) for _, device in others]
                if number == 2:
                    targets += [(index, device) for _, device in along_column]
                for slot, device in targets:
                    copy = message(slots.at[number, index], number, slot, len(started), device)
                    copy.start()
                    started.append(copy)
                found = list(others)
                if number == 0:
                    found += [(4 + place_x, device) for place_x, device in along_row]
                total = gather(number, found, 8)
            whole[...] = total
            for copy in started:
                copy.wait_send()

        value = whole[...]
        for item in (down_z, up_z, *down_t, *up_t, edge_z, edge_t):
            guarded(item[1], item[0].wait_send)

    charge = jnp.zeros((1, 128), jnp.float32)
    for mode in range(MODES):
        charge = jnp.where(lane % 16 == mode, charge_ref[mode].astype(jnp.float32), charge)
    charge = charge / 3.0
    volume = 24.0 * SITES * (2 * n_gz)
    scale = jnp.where(
        lane < 64, 1.0 / math.sqrt(volume * lattice_t), 1.0 / math.sqrt(volume * TW)
    )
    scale = scale * jnp.where(lane // 16 % 2 == 0, charge, charge * charge)
    out_ref[...] = value * scale


def insert_sums(counts, comm, low, links, photon, charges, start):
    vmem = pl.BlockSpec(memory_space=pltpu.VMEM)
    return pl.pallas_call(
        functools.partial(hop_kernel, counts, comm),
        out_shape=pltpu.VMEM((MODES, 128), jnp.float32),
        in_specs=[pl.BlockSpec(memory_space=pl.ANY)] * 6,
        out_specs=vmem,
        scratch_shapes=[
            pltpu.SMEM(start.shape, start.dtype),
            pltpu.SMEM(charges.shape, charges.dtype),
            pltpu.VMEM(low.shape, low.dtype),
            pltpu.VMEM(links.shape, links.dtype),
            pltpu.VMEM(photon.shape, photon.dtype),
            pltpu.VMEM((1536, 128), jnp.bfloat16),
            pltpu.VMEM((4, 4, SC, 32, SITES), jnp.bfloat16),
            pltpu.VMEM((ROWS, 2 * SITES), jnp.float32),
            pltpu.VMEM((ROWS, 2 * SITES), jnp.float32),
            pltpu.VMEM((SITES, 2 * SITES), jnp.bfloat16),
            pltpu.VMEM((7, 72, 8, SITES), jnp.float32),
            pltpu.VMEM((7, 4, 8, SITES), jnp.float32),
            pltpu.VMEM((3, EDGE, SITES), jnp.float32),
            pltpu.VMEM((3, EDGE, SITES), jnp.float32),
            pltpu.VMEM((256, SC * 128), jnp.bfloat16),
            pltpu.VMEM((256, SC * 128), jnp.bfloat16),
            pltpu.VMEM((128, SC * SITES), jnp.bfloat16),
            pltpu.VMEM((128, SC * SITES), jnp.bfloat16),
            pltpu.VMEM((2, 2, 32, 128), jnp.float32),
            pltpu.VMEM((8, 2, 64, 64), jnp.float32),
            pltpu.VMEM((MODES, 128), jnp.float32),
            pltpu.VMEM((3, 8, MODES, 128), jnp.float32),
            pltpu.VMEM((MODES, 128), jnp.float32),
            pltpu.SemaphoreType.DMA((6,)),
            pltpu.SemaphoreType.DMA((8,)),
            pltpu.SemaphoreType.DMA((8,)),
            pltpu.SemaphoreType.DMA((25,)),
            pltpu.SemaphoreType.DMA((3, 8)),
        ],
        compiler_params=pltpu.CompilerParams(
            collective_id=0 if comm else None,
            has_side_effects=comm,
            vmem_limit_bytes=60 * 1024 * 1024,
        ),
    )(start, charges, low, links, photon, jnp.asarray(fold_table(), jnp.bfloat16))


def lay_out(sums, *outputs):
    for window in range(2):
        for part in range(2):
            for order in range(2):
                start = window * 64 + part * 32 + order * 16
                outputs[window * 2 + order][part] = sums[:, start : start + 16]


def per_device(counts, comm, low_modes, gauge_links, photon, charges, window_start):
    sums = insert_sums(counts, comm, low_modes, gauge_links, photon, charges, window_start)
    vmem = pl.BlockSpec(memory_space=pltpu.VMEM)
    return pl.pallas_call(
        lay_out,
        out_shape=[jax.ShapeDtypeStruct((2, MODES, MODES), jnp.float32)] * 4,
        in_specs=[vmem],
        out_specs=[vmem] * 4,
    )(sums)


def solution(mesh):
    counts = (mesh.shape["gz"], mesh.shape["ta"])
    return jax.shard_map(
        functools.partial(per_device, counts, True),
        mesh=mesh,
        in_specs=(
            P(None, None, None, None, "ta", "gz", None),
            P(None, None, "ta", "gz", None),
            P(None, "ta", "gz", None),
            P(),
            P(),
        ),
        out_specs=(P(), P(), P(), P()),
        check_vma=False,
    )
```

```python
import functools
import math

import jax
import jax.numpy as jnp
import numpy as np
from jax import lax
from jax.experimental import pallas as pl
from jax.experimental.pallas import tpu as pltpu
from jax.sharding import PartitionSpec as P

LY = 16
TW = 4
MODES = 16
SC = 12
SITES = 256
ROWS = SC * 32
EDGE = 24
MESH = pl.DeviceIdType.MESH

GAMMA = (
    ((3, 0, 1), (2, 0, 1), (1, 0, -1), (0, 0, -1)),
    ((3, -1, 0), (2, 1, 0), (1, 1, 0), (0, -1, 0)),
    ((2, 0, 1), (3, 0, -1), (0, 0, -1), (1, 0, 1)),
)


def fold_table():
    table = np.zeros((1536, 128), np.float32)

    def put(row, ket, order, plain, value):
        for side in range(2):
            factor = value * (0.5 if order == 0 else 0.25)
            if side == 0:
                factor = factor if plain else -factor
                factor = factor * (-1j if order == 0 else 1)
                parts = (factor.real, factor.imag)
            else:
                factor = np.conj(factor) * (1j if order == 0 else 1)
                parts = (factor.real, factor.imag)
            for part in range(2):
                table[row, side * 64 + part * 32 + order * 16 + ket] += parts[part]

    for bra in range(2):
        for half in range(2):
            for low in range(2):
                for part in range(2):
                    for mode in range(8):
                        ket = half * 8 + mode
                        value = (1, -1j)[bra] * (1, 1j)[part]
                        tail = low * 16 + part * 8 + mode
                        for kind in range(4):
                            row = bra * 256 + half * 128 + kind * 32 + tail
                            put(row, ket, kind // 2, kind % 2 == 0, value)
                        for order in range(2):
                            for turned in range(2):
                                row = (turned * 2 + bra) * 128 + half * 64 + order * 32 + tail
                                put(512 + row, ket, order, turned == 0, value)
                                phase = 1j if turned else 1
                                put(1024 + row, ket, order, turned == 0, value * phase)
    return table


def split(value):
    high = value.astype(jnp.bfloat16)
    low = (value - high.astype(jnp.float32)).astype(jnp.bfloat16)
    return high, low


def colour_row(rows, vectors):
    result = []
    for spin in range(4):
        total_re = None
        total_im = None
        for b in range(3):
            ur, ui = rows[b]
            value = vectors(spin * 3 + b)
            vr, vi = value[:8], value[8:]
            re = ur * vr - ui * vi
            im = ur * vi + ui * vr
            total_re = re if total_re is None else total_re + re
            total_im = im if total_im is None else total_im + im
        result.append((total_re, total_im))
    return result


def times(entry, pair):
    _, re, im = entry
    if re:
        return (re, pair[0]), (re, pair[1])
    return (-im, pair[1]), (im, pair[0])


def add_signed(total, sign, value):
    if total is None:
        return value if sign > 0 else -value
    return total + value if sign > 0 else total - value


def link_rows(links, slot, base, a, lanes):
    return [
        (links[slot, base + a * 3 + b, :, lanes], links[slot, base + 9 + a * 3 + b, :, lanes])
        for b in range(3)
    ]


def store_pair(ket, row, column, pair):
    high, low = split(jnp.concatenate(pair, axis=0))
    ket[row : row + 16, column : column + 128] = high
    ket[row + 16 : row + 32, column : column + 128] = low


def space_unit(t, zz, lane, half, vall, vxy, links, field, ket):
    lanes = slice(lane * 128, lane * 128 + 128)
    slot = t * 2 + zz

    def from_x(sc):
        return vxy[sc * 32 + half * 16 : sc * 32 + half * 16 + 16, lanes]

    def from_y(sc):
        row = sc * 32 + half * 16
        return vxy[row : row + 16, SITES + lane * 128 : SITES + lane * 128 + 128]

    def from_z(sc):
        rows = slice(half * 16, half * 16 + 16)
        return vall[t + 1, zz + 2, sc, rows, lanes].astype(jnp.float32)

    sources = (from_x, from_y, from_z) if zz == 0 else (from_x, from_y)
    for a in range(3):
        hops = [
            colour_row(link_rows(links, slot, mu * 18, a, lanes), source)
            for mu, source in enumerate(sources)
        ]
        for order in range(2):
            if order == 1:
                for mu in range(len(hops)):
                    photon = field[slot, mu, :, lanes]
                    hops[mu] = [(photon * re, photon * im) for re, im in hops[mu]]
            for spin in range(4):
                plain = [None, None]
                crossed = [None, None]
                for mu, hopped in enumerate(hops):
                    entry = GAMMA[mu][spin]
                    turned = times(entry, hopped[entry[0]])
                    for part in range(2):
                        plain[part] = add_signed(plain[part], 1, hopped[spin][part])
                        crossed[part] = add_signed(crossed[part], *turned[part])
                column = (spin * 3 + a) * 128
                store_pair(ket, half * 128 + order * 64, column, plain)
                store_pair(ket, half * 128 + order * 64 + 32, column, crossed)


def space_product(t, zz, lane, chunk, vall, ket):
    lanes = slice(lane * 128, lane * 128 + 128)
    scs = range(chunk * 6, chunk * 6 + 6)
    bra = jnp.concatenate([vall[t + 1, zz + 1, sc, :, lanes] for sc in scs], axis=1)
    return [
        lax.dot_general(
            bra,
            ket[half * 128 : half * 128 + 128, chunk * 768 : chunk * 768 + 768],
            (((1,), (1,)), ((), ())),
            preferred_element_type=jnp.float32,
        )
        for half in range(2)
    ]


def link_unit(up, slot, mu, lane, half, vall, links, field, ket):
    lanes = slice(lane * 128, lane * 128 + 128)

    def source(sc):
        return vall[up[0], up[1], sc, half * 16 : half * 16 + 16, lanes].astype(jnp.float32)

    photon = field[slot, mu, :, lanes]
    for a in range(3):
        first = colour_row(link_rows(links, slot, mu * 18, a, lanes), source)
        for spin in range(4):
            re, im = first[spin]
            column = (spin * 3 + a) * SITES + lane * 128
            store_pair(ket, half * 64, column, (re, im))
            store_pair(ket, half * 64 + 32, column, (photon * re, photon * im))


def link_product(low, sign, chunk, vall, ket):
    scs = range(chunk * 3, chunk * 3 + 3)
    pieces = [vall[low[0], low[1], sc] for sc in scs]
    turned = [vall[low[0], low[1], (sc + 6) % SC] for sc in scs]
    if chunk in (0, 3):
        turned = [piece * sign for piece in turned]
    bra = jnp.concatenate(
        [jnp.concatenate(pieces, axis=1), jnp.concatenate(turned, axis=1)], axis=0
    )
    return [
        lax.dot_general(
            bra,
            ket[half * 64 : half * 64 + 64, chunk * 768 : chunk * 768 + 768],
            (((1,), (1,)), ((), ())),
            preferred_element_type=jnp.float32,
        )
        for half in range(2)
    ]


def plus(totals, parts):
    if totals is None:
        return parts
    return [total + part for total, part in zip(totals, parts)]


def hop_kernel(
    counts,
    comm,
    start_hbm,
    charge_hbm,
    low_ref,
    link_ref,
    photon_ref,
    table_ref,
    out_ref,
    start_ref,
    charge_ref,
    raw,
    raw_links,
    raw_photon,
    table,
    vall,
    vxy_a,
    vxy_b,
    perm,
    links,
    field,
    edge_out,
    edge_in,
    ket_s0,
    ket_s1,
    ket_p0,
    ket_p1,
    acc_s,
    acc_p,
    share,
    slots,
    whole,
    local_sem,
    send_sem,
    recv_sem,
    sum_send,
    sum_recv,
):
    n_gz, n_ta = counts
    own = [
        pltpu.make_async_copy(src, dst, local_sem.at[number])
        for number, (src, dst) in enumerate(
            (
                (low_ref, raw),
                (link_ref, raw_links),
                (photon_ref, raw_photon),
                (table_ref, table),
                (start_hbm, start_ref),
                (charge_hbm, charge_ref),
            )
        )
    ]
    for copy in own:
        copy.start()

    if comm:
        gz, ta = lax.axis_index("gz"), lax.axis_index("ta")
    else:
        gz, ta = jnp.int32(0), jnp.int32(0)

    def at(g, t):
        return {"gz": g, "ta": t}

    def wrapped(value, count):
        return jnp.where(value >= count, value - count, value)

    z_hi = lax.div(gz, 4)
    x = gz - z_hi * 4
    y = lax.div(ta, 4)
    inner = ta - y * 4
    z_lo = lax.div(inner, 2)
    core = inner - z_lo * 2
    z = z_hi * 2 + z_lo

    others_x, others_z, others_y = [], [], []
    for dx in (2, 1, 3):
        peer_x = wrapped(x + dx, 4)
        others_x.append((peer_x, at(z_hi * 4 + peer_x, ta)))
    for dz in (2, 1, 3, 0):
        peer_hi = wrapped(z_hi + dz, 4) if dz else z_hi
        for peer_lo in (z_lo, 1 - z_lo):
            if dz or peer_lo is not z_lo:
                others_z.append(
                    (peer_hi * 2 + peer_lo, at(peer_hi * 4 + x, ta + (peer_lo - z_lo) * 2))
                )
    for dy in (4, 3, 5, 2, 6, 1, 7):
        peer_y = wrapped(y + dy, 8)
        others_y.append((peer_y, at(gz, peer_y * 4 + inner)))
    stages = ((others_x, x), (others_z, z), (others_y, y))
    crossed = ta + 1 - 2 * core
    along_row = [(x, at(gz, crossed))]
    along_row += [
        (wrapped(x + dx, 4), at(z_hi * 4 + wrapped(x + dx, 4), crossed)) for dx in (2, 1, 3)
    ]
    along_column = [(y, at(gz, crossed))]
    along_column += [
        (wrapped(y + dy, 8), at(gz, wrapped(y + dy, 8) * 4 + crossed - y * 4))
        for dy in (4, 3, 5, 2, 6, 1, 7)
    ]
    is_first, is_second = core == 0, core == 1

    below_z = at(jnp.where(gz == 0, n_gz - 1, gz - 1), ta)
    above_z = at(wrapped(gz + 1, n_gz), ta)
    below_t = at(gz, jnp.where(ta == 0, n_ta - 1, ta - 1))
    above_t = at(gz, wrapped(ta + 1, n_ta))

    first_kind = z_lo == 0
    upper_up = jnp.logical_and(
        core == 1,
        jnp.logical_or(
            jnp.logical_and(x == 0, first_kind),
            jnp.logical_and(x == 3, jnp.logical_not(first_kind)),
        ),
    )
    lower_up = jnp.logical_and(
        core == 0,
        jnp.logical_or(
            jnp.logical_and(x == 0, jnp.logical_not(first_kind)),
            jnp.logical_and(x == 3, first_kind),
        ),
    )
    upper_down = jnp.logical_not(upper_up)
    lower_down = jnp.logical_not(lower_up)
    always = None

    barrier = pltpu.get_barrier_semaphore() if comm else None
    if comm:
        greeted = [below_z, above_z, below_t, above_t]
        greeted += [device for _, device in along_row + along_column]
        for device in greeted:
            pl.semaphore_signal(barrier, inc=1, device_id=device, device_id_type=MESH)

        @pl.when(is_second)
        def _():
            for group, _ in stages:
                for _, device in group:
                    pl.semaphore_signal(barrier, inc=1, device_id=device, device_id_type=MESH)

    def copy_to(src, dst, which, device):
        if comm:
            return pltpu.make_async_remote_copy(
                src_ref=src,
                dst_ref=dst,
                send_sem=send_sem.at[which],
                recv_sem=recv_sem.at[which],
                device_id=device,
                device_id_type=MESH,
            )
        return pltpu.make_async_copy(src, dst, recv_sem.at[which])

    down_z = (copy_to(vall.at[1, 1], vall.at[1, 3], 0, below_z), always, always)
    up_z = (copy_to(vall.at[2, 2], vall.at[2, 0], 1, above_z), always, always)
    down_t = [
        (copy_to(vall.at[1, zz + 1], vall.at[3, zz + 1], 2 + zz, below_t), lower_down, upper_down)
        for zz in range(2)
    ]
    up_t = [
        (copy_to(vall.at[2, zz + 1], vall.at[0, zz + 1], 4 + zz, above_t), upper_up, lower_up)
        for zz in range(2)
    ]
    edge_z = (copy_to(edge_out.at[0], edge_in.at[0], 6, above_z), always, always)
    edge_t = (
        copy_to(edge_out.at[pl.ds(1, 2)], edge_in.at[pl.ds(1, 2)], 7, above_t),
        upper_up,
        lower_up,
    )

    def guarded(flag, action):
        if flag is None:
            action()
        else:
            pl.when(flag)(action)

    def start(item):
        guarded(item[1], item[0].start)

    def arrive(item):
        guarded(item[2], item[0].wait_recv if comm else item[0].wait)

    row = lax.broadcasted_iota(jnp.int32, (SITES, SITES), 0)
    column = lax.broadcasted_iota(jnp.int32, (SITES, SITES), 1)
    along_x = (column + LY) % SITES
    along_y = (column - column % LY) + (column + 1) % LY
    perm[:, :SITES] = (row == along_x).astype(jnp.float32).astype(jnp.bfloat16)
    perm[:, SITES:] = (row == along_y).astype(jnp.float32).astype(jnp.bfloat16)
    acc_s[...] = jnp.zeros_like(acc_s)
    acc_p[...] = jnp.zeros_like(acc_p)
    ket_s1[...] = jnp.zeros_like(ket_s1)
    ket_p1[...] = jnp.zeros_like(ket_p1)

    def arrange(t):
        def one_spin(spin, _):
            for colour in range(3):
                parts = [
                    jnp.swapaxes(raw[:, part, spin, colour, t].astype(jnp.float32), 0, 1)
                    for part in range(2)
                ]
                for zz in range(2):
                    for half in range(2):
                        vall[
                            t + 1, zz + 1, spin * 3 + colour, half * 16 : half * 16 + 16, :
                        ] = jnp.concatenate(
                            [part[zz, half * 8 : half * 8 + 8] for part in parts], axis=0
                        ).astype(jnp.bfloat16)
            return 0

        lax.fori_loop(0, 4, one_spin, 0)

    own[0].wait()
    arrange(0)
    if comm:
        pl.semaphore_wait(barrier, jnp.where(is_second, 33, 16))
    for item in (down_z, *down_t):
        start(item)
    arrange(1)
    for item in (up_z, *up_t):
        start(item)

    own[1].wait()
    own[2].wait()

    def spread(t, _):
        turn = jnp.where(jnp.logical_and(ta == n_ta - 1, t == 1), -1.0, 1.0)
        for mu in range(4):
            photon = raw_photon[mu, t]
            scale = photon * turn if mu == 3 else photon
            for zz in range(2):
                field[t * 2 + zz, mu] = jnp.broadcast_to(photon[zz : zz + 1], (8, SITES))
            for entry in range(18):
                scaled = raw_links[mu, entry, t] * scale
                for zz in range(2):
                    links[t * 2 + zz, mu * 18 + entry] = jnp.broadcast_to(
                        scaled[zz : zz + 1], (8, SITES)
                    )
        return 0

    lax.fori_loop(0, 2, spread, 0)

    for number, (slot, mu) in enumerate(((3, 2), (2, 3), (3, 3))):
        rows = [links[slot, mu * 18 + entry, 0:1] for entry in range(18)]
        rows.append(field[slot, mu, 0:1])
        rows.append(jnp.zeros((EDGE - 19, SITES), jnp.float32))
        edge_out[number] = jnp.concatenate(rows, axis=0)
    start(edge_z)
    start(edge_t)

    def shift(t, zz, vxy):
        vxy[...] = jnp.dot(
            vall[t + 1, zz + 1].reshape(ROWS, SITES),
            perm[...],
            preferred_element_type=jnp.float32,
        )

    def shift_half(t, zz, vxy, part):
        vxy[part * 192 : part * 192 + 192, :] = jnp.dot(
            vall[t + 1, zz + 1, part * 6 : part * 6 + 6].reshape(192, SITES),
            perm[...],
            preferred_element_type=jnp.float32,
        )

    shift(0, 0, vxy_a)

    def blocks(t, _):
        kets = (ket_s0, ket_s1)
        pending = (jnp.maximum(t - 1, 0), 1, 1)
        for zz, vxy in ((0, vxy_a), (1, vxy_b)):
            for lane in range(2):

                @pl.when(core >= 0)
                def _(zz=zz, vxy=vxy, lane=lane, pending=pending):
                    totals = None
                    for half in range(2):
                        space_unit(t, zz, lane, half, vall, vxy, links, field, kets[lane])
                        totals = plus(totals, space_product(*pending, half, vall, kets[pending[2]]))
                    for half in range(2):
                        acc_s[pending[0], half] += totals[half]
                    if zz == 0:
                        shift_half(t, 1, vxy_b, lane)
                    else:
                        shift_half(jnp.minimum(t + 1, 1), 0, vxy_a, lane)

                pending = (t, zz, lane)
        return 0

    lax.fori_loop(0, 2, blocks, 0)
    for chunk in range(2):
        for half, part in enumerate(space_product(1, 1, 1, chunk, vall, ket_s1)):
            acc_s[1, half] += part

    def spread_edge(number, slot, mu):
        for entry in range(18):
            links[slot, mu * 18 + entry] = jnp.broadcast_to(
                edge_in[number, entry : entry + 1], (8, SITES)
            )
        field[slot, mu] = jnp.broadcast_to(edge_in[number, 18:19], (8, SITES))

    z_first = jnp.where(x == 0, 0, 1)

    def place(number, which):
        z_t = z_first if which == 0 else 1 - z_first
        is_z = number == 3
        low_t = lax.rem(number + 1, 3)
        low = (jnp.where(is_z, z_t + 1, low_t), jnp.where(is_z, 2 - 2 * z_t, which + 1))
        up = (jnp.where(is_z, z_t + 1, low_t + 1), jnp.where(is_z, 3 - 2 * z_t, which + 1))
        slot = jnp.where(
            is_z, 1 + 3 * z_t, jnp.where(number == 2, 5, number * 2) + which
        )
        product = number * 2 + jnp.where(is_z, z_t, which)
        sign = jnp.where(is_z, -1.0, 1.0).astype(jnp.bfloat16)
        return low, up, slot, product, sign, z_t

    def product_of(number, which, ket, units=None):
        low, _, _, product, sign, _ = place(number, which)
        totals = None
        for chunk in range(4):
            if units is not None:
                units(chunk)
            totals = plus(totals, link_product(low, sign, chunk, vall, ket))
        for half in range(2):
            acc_p[product, half] = totals[half]

    def pair(number, previous):
        is_z = number == 3
        active = jnp.logical_or(
            jnp.logical_or(number == 0, is_z),
            jnp.logical_or(
                jnp.logical_and(number == 1, upper_down), jnp.logical_and(number == 2, lower_up)
            ),
        )

        @pl.when(active)
        def _():
            for which, ket in enumerate((ket_p0, ket_p1)):
                _, up, slot, _, _, z_t = place(number, which)

                @pl.when(number == 1)
                def _():
                    arrive(down_t[which])

                @pl.when(number == 2)
                def _():
                    arrive(up_t[which])
                    if which == 0:
                        arrive(edge_t)

                    @pl.when(lower_up)
                    def _():
                        spread_edge(1 + which, 5 + which, 3)

                @pl.when(jnp.logical_and(is_z, z_t == 0))
                def _():
                    arrive(down_z)

                @pl.when(jnp.logical_and(is_z, z_t == 1))
                def _():
                    arrive(up_z)
                    arrive(edge_z)
                    spread_edge(0, 4, 2)

                mu = jnp.where(is_z, 2, 3)

                def units(step, up=up, slot=slot, ket=ket):
                    link_unit(up, slot, mu, step // 2, step % 2, vall, links, field, ket)

                if which == 0:
                    product_of(previous, 1, ket_p1, units)
                else:
                    product_of(number, 0, ket_p0, units)

        return jnp.where(active, number, previous)

    lax.fori_loop(0, 4, pair, jnp.int32(0))
    product_of(jnp.int32(3), 1, ket_p1)

    own[4].wait()
    begin = start_ref[0]
    lattice_t = 2 * n_ta

    def inside(t):
        offset = (ta * 2 + t - begin + 2 * lattice_t) % lattice_t
        return jnp.where(offset < TW, 1.0, 0.0)

    before, first_in, last_in, after = (inside(t) for t in (-1, 0, 1, 2))

    def by_part(values, groups):
        rows = []
        for group in range(groups):
            for part in range(2):
                base = group * 32 + part * 8
                rows.append(
                    jnp.concatenate([values[base : base + 8], values[base + 16 : base + 24]], axis=0)
                )
        return jnp.concatenate(rows, axis=1)

    def both(acc, index):
        return jnp.concatenate([acc[index, 0], acc[index, 1]], axis=1)

    spaces = [by_part(both(acc_s, t), 1) for t in range(2)]
    times_in, times_up, times_low = (
        by_part(both(acc_p, 2 * number) + both(acc_p, 2 * number + 1), 2) for number in range(3)
    )
    z_links = [by_part(both(acc_p, 6 + t), 2) for t in range(2)]
    space_in = first_in * spaces[0] + last_in * spaces[1]
    z_in = first_in * z_links[0] + last_in * z_links[1]
    products = jnp.concatenate(
        [
            jnp.concatenate(
                [spaces[0] + spaces[1], times_in + times_up + times_low, z_links[0] + z_links[1]],
                axis=1,
            ),
            jnp.concatenate(
                [
                    space_in,
                    first_in * times_in + last_in * times_up + before * times_low,
                    z_in,
                ],
                axis=1,
            ),
            jnp.concatenate(
                [
                    space_in,
                    last_in * times_in + after * times_up + first_in * times_low,
                    z_in,
                ],
                axis=1,
            ),
        ],
        axis=0,
    )
    own[3].wait()
    own[5].wait()
    high, rest = split(products)
    middle, low = split(products - high.astype(jnp.float32))
    folded = jnp.dot(
        jnp.concatenate([high, middle, low], axis=0),
        table[...],
        preferred_element_type=jnp.float32,
    )
    folded = folded[:48] + folded[48:96] + folded[96:]
    lane = lax.broadcasted_iota(jnp.int32, (1, 128), 1)
    windowed = jnp.where(lane < 64, folded[16:32], folded[32:])
    backward = jnp.transpose(jnp.concatenate([folded[:16], windowed], axis=0))[64:]
    pieces = [
        backward[group * 16 : group * 16 + 16, window * 16 : window * 16 + 16]
        for window in range(2)
        for group in range(4)
    ]
    value = jnp.concatenate([folded[:16, :64], windowed[:, :64]], axis=1)
    value = value + jnp.concatenate(pieces, axis=1)

    if comm:

        def message(src, number, slot, sent, device):
            return pltpu.make_async_remote_copy(
                src_ref=src,
                dst_ref=slots.at[number, slot],
                send_sem=sum_send.at[sent],
                recv_sem=sum_recv.at[number, slot],
                device_id=device,
                device_id_type=MESH,
            )

        def gather(number, found, last):
            for slot, device in found:
                message(slots.at[number, slot], number, slot, 0, device).wait_recv()
            total = slots[number, 0]
            for other in range(1, last):
                total = total + slots[number, other]
            return total

        @pl.when(is_first)
        def _():
            share[...] = value
            started = [
                message(share, 0, 4 + x, step, device)
                for step, (_, device) in enumerate(along_row)
            ]
            for copy in started:
                copy.start()
            whole[...] = gather(2, along_column, 8)
            for copy in started:
                copy.wait_send()

        @pl.when(is_second)
        def _():
            total = value
            started = []
            for number, (others, index) in enumerate(stages):
                slots[number, index] = total
                targets = [(index, device) for _, device in others]
                if number == 2:
                    targets += [(index, device) for _, device in along_column]
                for slot, device in targets:
                    copy = message(slots.at[number, index], number, slot, len(started), device)
                    copy.start()
                    started.append(copy)
                found = list(others)
                if number == 0:
                    found += [(4 + place_x, device) for place_x, device in along_row]
                total = gather(number, found, 8)
            whole[...] = total
            for copy in started:
                copy.wait_send()

        value = whole[...]
        for item in (down_z, up_z, *down_t, *up_t, edge_z, edge_t):
            guarded(item[1], item[0].wait_send)

    charge = jnp.zeros((1, 128), jnp.float32)
    for mode in range(MODES):
        charge = jnp.where(lane % 16 == mode, charge_ref[mode].astype(jnp.float32), charge)
    charge = charge / 3.0
    volume = 24.0 * SITES * (2 * n_gz)
    scale = jnp.where(
        lane < 64, 1.0 / math.sqrt(volume * lattice_t), 1.0 / math.sqrt(volume * TW)
    )
    scale = scale * jnp.where(lane // 16 % 2 == 0, charge, charge * charge)
    out_ref[...] = value * scale


def insert_sums(counts, comm, low, links, photon, charges, start):
    vmem = pl.BlockSpec(memory_space=pltpu.VMEM)
    return pl.pallas_call(
        functools.partial(hop_kernel, counts, comm),
        out_shape=pltpu.VMEM((MODES, 128), jnp.float32),
        in_specs=[pl.BlockSpec(memory_space=pl.ANY)] * 6,
        out_specs=vmem,
        scratch_shapes=[
            pltpu.SMEM(start.shape, start.dtype),
            pltpu.SMEM(charges.shape, charges.dtype),
            pltpu.VMEM(low.shape, low.dtype),
            pltpu.VMEM(links.shape, links.dtype),
            pltpu.VMEM(photon.shape, photon.dtype),
            pltpu.VMEM((1536, 128), jnp.bfloat16),
            pltpu.VMEM((4, 4, SC, 32, SITES), jnp.bfloat16),
            pltpu.VMEM((ROWS, 2 * SITES), jnp.float32),
            pltpu.VMEM((ROWS, 2 * SITES), jnp.float32),
            pltpu.VMEM((SITES, 2 * SITES), jnp.bfloat16),
            pltpu.VMEM((7, 72, 8, SITES), jnp.float32),
            pltpu.VMEM((7, 4, 8, SITES), jnp.float32),
            pltpu.VMEM((3, EDGE, SITES), jnp.float32),
            pltpu.VMEM((3, EDGE, SITES), jnp.float32),
            pltpu.VMEM((256, SC * 128), jnp.bfloat16),
            pltpu.VMEM((256, SC * 128), jnp.bfloat16),
            pltpu.VMEM((128, SC * SITES), jnp.bfloat16),
            pltpu.VMEM((128, SC * SITES), jnp.bfloat16),
            pltpu.VMEM((2, 2, 32, 128), jnp.float32),
            pltpu.VMEM((8, 2, 64, 64), jnp.float32),
            pltpu.VMEM((MODES, 128), jnp.float32),
            pltpu.VMEM((3, 8, MODES, 128), jnp.float32),
            pltpu.VMEM((MODES, 128), jnp.float32),
            pltpu.SemaphoreType.DMA((6,)),
            pltpu.SemaphoreType.DMA((8,)),
            pltpu.SemaphoreType.DMA((8,)),
            pltpu.SemaphoreType.DMA((25,)),
            pltpu.SemaphoreType.DMA((3, 8)),
        ],
        compiler_params=pltpu.CompilerParams(
            collective_id=0 if comm else None,
            has_side_effects=comm,
            vmem_limit_bytes=60 * 1024 * 1024,
        ),
    )(start, charges, low, links, photon, jnp.asarray(fold_table(), jnp.bfloat16))


def lay_out(sums, *outputs):
    for window in range(2):
        for part in range(2):
            for order in range(2):
                start = window * 64 + part * 32 + order * 16
                outputs[window * 2 + order][part] = sums[:, start : start + 16]


def per_device(counts, comm, low_modes, gauge_links, photon, charges, window_start):
    sums = insert_sums(counts, comm, low_modes, gauge_links, photon, charges, window_start)
    vmem = pl.BlockSpec(memory_space=pltpu.VMEM)
    return pl.pallas_call(
        lay_out,
        out_shape=[jax.ShapeDtypeStruct((2, MODES, MODES), jnp.float32)] * 4,
        in_specs=[vmem],
        out_specs=[vmem] * 4,
        compiler_params=pltpu.CompilerParams(vmem_limit_bytes=1024 * 1024),
    )(sums)


def solution(mesh):
    counts = (mesh.shape["gz"], mesh.shape["ta"])
    return jax.shard_map(
        functools.partial(per_device, counts, True),
        mesh=mesh,
        in_specs=(
            P(None, None, None, None, "ta", "gz", None),
            P(None, None, "ta", "gz", None),
            P(None, "ta", "gz", None),
            P(),
            P(),
        ),
        out_specs=(P(), P(), P(), P()),
        check_vma=False,
    )
```

```python
import functools
import math

import jax
import jax.numpy as jnp
import numpy as np
from jax import lax
from jax.experimental import pallas as pl
from jax.experimental.pallas import tpu as pltpu
from jax.sharding import PartitionSpec as P

LY = 16
TW = 4
MODES = 16
SC = 12
SITES = 256
ROWS = SC * 32
EDGE = 24
MESH = pl.DeviceIdType.MESH

GAMMA = (
    ((3, 0, 1), (2, 0, 1), (1, 0, -1), (0, 0, -1)),
    ((3, -1, 0), (2, 1, 0), (1, 1, 0), (0, -1, 0)),
    ((2, 0, 1), (3, 0, -1), (0, 0, -1), (1, 0, 1)),
)


def fold_table():
    table = np.zeros((1536, 128), np.float32)

    def put(row, ket, order, plain, value):
        for side in range(2):
            factor = value * (0.5 if order == 0 else 0.25)
            if side == 0:
                factor = factor if plain else -factor
                factor = factor * (-1j if order == 0 else 1)
                parts = (factor.real, factor.imag)
            else:
                factor = np.conj(factor) * (1j if order == 0 else 1)
                parts = (factor.real, factor.imag)
            for part in range(2):
                table[row, side * 64 + part * 32 + order * 16 + ket] += parts[part]

    for bra in range(2):
        for half in range(2):
            for low in range(2):
                for part in range(2):
                    for mode in range(8):
                        ket = half * 8 + mode
                        value = (1, -1j)[bra] * (1, 1j)[part]
                        tail = low * 16 + part * 8 + mode
                        for kind in range(4):
                            row = bra * 256 + half * 128 + kind * 32 + tail
                            put(row, ket, kind // 2, kind % 2 == 0, value)
                        for order in range(2):
                            for turned in range(2):
                                row = (turned * 2 + bra) * 128 + half * 64 + order * 32 + tail
                                put(512 + row, ket, order, turned == 0, value)
                                phase = 1j if turned else 1
                                put(1024 + row, ket, order, turned == 0, value * phase)
    return table


def split(value):
    high = value.astype(jnp.bfloat16)
    low = (value - high.astype(jnp.float32)).astype(jnp.bfloat16)
    return high, low


def colour_row(rows, vectors):
    result = []
    for spin in range(4):
        total_re = None
        total_im = None
        for b in range(3):
            ur, ui = rows[b]
            value = vectors(spin * 3 + b)
            vr, vi = value[:8], value[8:]
            re = ur * vr - ui * vi
            im = ur * vi + ui * vr
            total_re = re if total_re is None else total_re + re
            total_im = im if total_im is None else total_im + im
        result.append((total_re, total_im))
    return result


def times(entry, pair):
    _, re, im = entry
    if re:
        return (re, pair[0]), (re, pair[1])
    return (-im, pair[1]), (im, pair[0])


def add_signed(total, sign, value):
    if total is None:
        return value if sign > 0 else -value
    return total + value if sign > 0 else total - value


def link_rows(links, slot, base, a, lanes):
    return [
        (links[slot, base + a * 3 + b, :, lanes], links[slot, base + 9 + a * 3 + b, :, lanes])
        for b in range(3)
    ]


def store_pair(ket, row, column, pair):
    high, low = split(jnp.concatenate(pair, axis=0))
    ket[row : row + 16, column : column + 128] = high
    ket[row + 16 : row + 32, column : column + 128] = low


def space_unit(t, zz, lane, half, vall, vxy, links, field, ket):
    lanes = slice(lane * 128, lane * 128 + 128)
    slot = t * 2 + zz

    def from_x(sc):
        return vxy[sc * 32 + half * 16 : sc * 32 + half * 16 + 16, lanes]

    def from_y(sc):
        row = sc * 32 + half * 16
        return vxy[row : row + 16, SITES + lane * 128 : SITES + lane * 128 + 128]

    def from_z(sc):
        rows = slice(half * 16, half * 16 + 16)
        return vall[t + 1, zz + 2, sc, rows, lanes].astype(jnp.float32)

    sources = (from_x, from_y, from_z) if zz == 0 else (from_x, from_y)
    for a in range(3):
        hops = [
            colour_row(link_rows(links, slot, mu * 18, a, lanes), source)
            for mu, source in enumerate(sources)
        ]
        for order in range(2):
            if order == 1:
                for mu in range(len(hops)):
                    photon = field[slot, mu, :, lanes]
                    hops[mu] = [(photon * re, photon * im) for re, im in hops[mu]]
            for spin in range(4):
                plain = [None, None]
                crossed = [None, None]
                for mu, hopped in enumerate(hops):
                    entry = GAMMA[mu][spin]
                    turned = times(entry, hopped[entry[0]])
                    for part in range(2):
                        plain[part] = add_signed(plain[part], 1, hopped[spin][part])
                        crossed[part] = add_signed(crossed[part], *turned[part])
                column = (spin * 3 + a) * 128
                store_pair(ket, half * 128 + order * 64, column, plain)
                store_pair(ket, half * 128 + order * 64 + 32, column, crossed)


def space_product(t, zz, lane, chunk, vall, ket):
    lanes = slice(lane * 128, lane * 128 + 128)
    scs = range(chunk * 6, chunk * 6 + 6)
    bra = jnp.concatenate([vall[t + 1, zz + 1, sc, :, lanes] for sc in scs], axis=1)
    return [
        lax.dot_general(
            bra,
            ket[half * 128 : half * 128 + 128, chunk * 768 : chunk * 768 + 768],
            (((1,), (1,)), ((), ())),
            preferred_element_type=jnp.float32,
        )
        for half in range(2)
    ]


def link_unit(up, slot, mu, lane, half, vall, links, field, ket):
    lanes = slice(lane * 128, lane * 128 + 128)

    def source(sc):
        return vall[up[0], up[1], sc, half * 16 : half * 16 + 16, lanes].astype(jnp.float32)

    photon = field[slot, mu, :, lanes]
    for a in range(3):
        first = colour_row(link_rows(links, slot, mu * 18, a, lanes), source)
        for spin in range(4):
            re, im = first[spin]
            column = (spin * 3 + a) * SITES + lane * 128
            store_pair(ket, half * 64, column, (re, im))
            store_pair(ket, half * 64 + 32, column, (photon * re, photon * im))


def link_product(low, sign, chunk, vall, ket):
    scs = range(chunk * 3, chunk * 3 + 3)
    pieces = [vall[low[0], low[1], sc] for sc in scs]
    turned = [vall[low[0], low[1], (sc + 6) % SC] for sc in scs]
    if chunk in (0, 3):
        turned = [piece * sign for piece in turned]
    bra = jnp.concatenate(
        [jnp.concatenate(pieces, axis=1), jnp.concatenate(turned, axis=1)], axis=0
    )
    return [
        lax.dot_general(
            bra,
            ket[half * 64 : half * 64 + 64, chunk * 768 : chunk * 768 + 768],
            (((1,), (1,)), ((), ())),
            preferred_element_type=jnp.float32,
        )
        for half in range(2)
    ]


def plus(totals, parts):
    if totals is None:
        return parts
    return [total + part for total, part in zip(totals, parts)]


def hop_kernel(
    counts,
    comm,
    start_hbm,
    charge_hbm,
    low_ref,
    link_ref,
    photon_ref,
    table_ref,
    out_ref,
    start_ref,
    charge_ref,
    raw,
    raw_links,
    raw_photon,
    table,
    vall,
    vxy_a,
    vxy_b,
    perm,
    links,
    field,
    edge_out,
    edge_in,
    ket_s0,
    ket_s1,
    ket_p0,
    ket_p1,
    acc_s,
    acc_p,
    share,
    slots,
    whole,
    local_sem,
    send_sem,
    recv_sem,
    sum_send,
    sum_recv,
):
    n_gz, n_ta = counts
    own = [
        pltpu.make_async_copy(src, dst, local_sem.at[number])
        for number, (src, dst) in enumerate(
            (
                (low_ref, raw),
                (link_ref, raw_links),
                (photon_ref, raw_photon),
                (table_ref, table),
                (start_hbm, start_ref),
                (charge_hbm, charge_ref),
            )
        )
    ]
    for copy in own:
        copy.start()

    if comm:
        gz, ta = lax.axis_index("gz"), lax.axis_index("ta")
    else:
        gz, ta = jnp.int32(0), jnp.int32(0)

    def at(g, t):
        return {"gz": g, "ta": t}

    def wrapped(value, count):
        return jnp.where(value >= count, value - count, value)

    z_hi = lax.div(gz, 4)
    x = gz - z_hi * 4
    y = lax.div(ta, 4)
    inner = ta - y * 4
    z_lo = lax.div(inner, 2)
    core = inner - z_lo * 2
    z = z_hi * 2 + z_lo

    others_x, others_z, others_y = [], [], []
    for dx in (2, 1, 3):
        peer_x = wrapped(x + dx, 4)
        others_x.append((peer_x, at(z_hi * 4 + peer_x, ta)))
    for dz in (2, 1, 3, 0):
        peer_hi = wrapped(z_hi + dz, 4) if dz else z_hi
        for peer_lo in (z_lo, 1 - z_lo):
            if dz or peer_lo is not z_lo:
                others_z.append(
                    (peer_hi * 2 + peer_lo, at(peer_hi * 4 + x, ta + (peer_lo - z_lo) * 2))
                )
    for dy in (4, 3, 5, 2, 6, 1, 7):
        peer_y = wrapped(y + dy, 8)
        others_y.append((peer_y, at(gz, peer_y * 4 + inner)))
    stages = ((others_x, x), (others_z, z), (others_y, y))
    crossed = ta + 1 - 2 * core
    along_row = [
        (wrapped(x + dx, 4), at(z_hi * 4 + wrapped(x + dx, 4), crossed)) for dx in (2, 1, 3)
    ]
    along_row.append((x, at(gz, crossed)))
    along_column = [
        (wrapped(y + dy, 8), at(gz, wrapped(y + dy, 8) * 4 + crossed - y * 4))
        for dy in (4, 3, 5, 2, 6, 1, 7)
    ]
    along_column.append((y, at(gz, crossed)))
    is_first, is_second = core == 0, core == 1

    below_z = at(jnp.where(gz == 0, n_gz - 1, gz - 1), ta)
    above_z = at(wrapped(gz + 1, n_gz), ta)
    below_t = at(gz, jnp.where(ta == 0, n_ta - 1, ta - 1))
    above_t = at(gz, wrapped(ta + 1, n_ta))

    first_kind = z_lo == 0
    upper_up = jnp.logical_and(
        core == 1,
        jnp.logical_or(
            jnp.logical_and(x == 0, first_kind),
            jnp.logical_and(x == 3, jnp.logical_not(first_kind)),
        ),
    )
    lower_up = jnp.logical_and(
        core == 0,
        jnp.logical_or(
            jnp.logical_and(x == 0, jnp.logical_not(first_kind)),
            jnp.logical_and(x == 3, first_kind),
        ),
    )
    upper_down = jnp.logical_not(upper_up)
    lower_down = jnp.logical_not(lower_up)
    always = None

    barrier = pltpu.get_barrier_semaphore() if comm else None
    if comm:
        greeted = [below_z, above_z, below_t, above_t]
        greeted += [device for _, device in along_row + along_column]
        for device in greeted:
            pl.semaphore_signal(barrier, inc=1, device_id=device, device_id_type=MESH)

        @pl.when(is_second)
        def _():
            for group, _ in stages:
                for _, device in group:
                    pl.semaphore_signal(barrier, inc=1, device_id=device, device_id_type=MESH)

    def copy_to(src, dst, which, device):
        if comm:
            return pltpu.make_async_remote_copy(
                src_ref=src,
                dst_ref=dst,
                send_sem=send_sem.at[which],
                recv_sem=recv_sem.at[which],
                device_id=device,
                device_id_type=MESH,
            )
        return pltpu.make_async_copy(src, dst, recv_sem.at[which])

    down_z = (copy_to(vall.at[1, 1], vall.at[1, 3], 0, below_z), always, always)
    up_z = (copy_to(vall.at[2, 2], vall.at[2, 0], 1, above_z), always, always)
    down_t = [
        (copy_to(vall.at[1, zz + 1], vall.at[3, zz + 1], 2 + zz, below_t), lower_down, upper_down)
        for zz in range(2)
    ]
    up_t = [
        (copy_to(vall.at[2, zz + 1], vall.at[0, zz + 1], 4 + zz, above_t), upper_up, lower_up)
        for zz in range(2)
    ]
    edge_z = (copy_to(edge_out.at[0], edge_in.at[0], 6, above_z), always, always)
    edge_t = (
        copy_to(edge_out.at[pl.ds(1, 2)], edge_in.at[pl.ds(1, 2)], 7, above_t),
        upper_up,
        lower_up,
    )

    def guarded(flag, action):
        if flag is None:
            action()
        else:
            pl.when(flag)(action)

    def start(item):
        guarded(item[1], item[0].start)

    def arrive(item):
        guarded(item[2], item[0].wait_recv if comm else item[0].wait)

    row = lax.broadcasted_iota(jnp.int32, (SITES, SITES), 0)
    column = lax.broadcasted_iota(jnp.int32, (SITES, SITES), 1)
    along_x = (column + LY) % SITES
    along_y = (column - column % LY) + (column + 1) % LY
    perm[:, :SITES] = (row == along_x).astype(jnp.float32).astype(jnp.bfloat16)
    perm[:, SITES:] = (row == along_y).astype(jnp.float32).astype(jnp.bfloat16)
    acc_s[...] = jnp.zeros_like(acc_s)
    acc_p[...] = jnp.zeros_like(acc_p)
    ket_s1[...] = jnp.zeros_like(ket_s1)
    ket_p1[...] = jnp.zeros_like(ket_p1)

    def arrange(t):
        def one_spin(spin, _):
            for colour in range(3):
                parts = [
                    jnp.swapaxes(raw[:, part, spin, colour, t].astype(jnp.float32), 0, 1)
                    for part in range(2)
                ]
                for zz in range(2):
                    for half in range(2):
                        vall[
                            t + 1, zz + 1, spin * 3 + colour, half * 16 : half * 16 + 16, :
                        ] = jnp.concatenate(
                            [part[zz, half * 8 : half * 8 + 8] for part in parts], axis=0
                        ).astype(jnp.bfloat16)
            return 0

        lax.fori_loop(0, 4, one_spin, 0)

    own[0].wait()
    arrange(0)
    if comm:
        pl.semaphore_wait(barrier, jnp.where(is_second, 33, 16))
    for item in (down_z, *down_t):
        start(item)
    arrange(1)
    for item in (up_z, *up_t):
        start(item)

    own[1].wait()
    own[2].wait()

    def spread(t, _):
        turn = jnp.where(jnp.logical_and(ta == n_ta - 1, t == 1), -1.0, 1.0)
        for mu in range(4):
            photon = raw_photon[mu, t]
            scale = photon * turn if mu == 3 else photon
            for zz in range(2):
                field[t * 2 + zz, mu] = jnp.broadcast_to(photon[zz : zz + 1], (8, SITES))
            for entry in range(18):
                scaled = raw_links[mu, entry, t] * scale
                for zz in range(2):
                    links[t * 2 + zz, mu * 18 + entry] = jnp.broadcast_to(
                        scaled[zz : zz + 1], (8, SITES)
                    )
        return 0

    lax.fori_loop(0, 2, spread, 0)

    for number, (slot, mu) in enumerate(((3, 2), (2, 3), (3, 3))):
        rows = [links[slot, mu * 18 + entry, 0:1] for entry in range(18)]
        rows.append(field[slot, mu, 0:1])
        rows.append(jnp.zeros((EDGE - 19, SITES), jnp.float32))
        edge_out[number] = jnp.concatenate(rows, axis=0)
    start(edge_z)
    start(edge_t)

    def shift(t, zz, vxy):
        vxy[...] = jnp.dot(
            vall[t + 1, zz + 1].reshape(ROWS, SITES),
            perm[...],
            preferred_element_type=jnp.float32,
        )

    def shift_half(t, zz, vxy, part):
        vxy[part * 192 : part * 192 + 192, :] = jnp.dot(
            vall[t + 1, zz + 1, part * 6 : part * 6 + 6].reshape(192, SITES),
            perm[...],
            preferred_element_type=jnp.float32,
        )

    shift(0, 0, vxy_a)

    def blocks(t, _):
        kets = (ket_s0, ket_s1)
        pending = (jnp.maximum(t - 1, 0), 1, 1)
        for zz, vxy in ((0, vxy_a), (1, vxy_b)):
            for lane in range(2):

                @pl.when(core >= 0)
                def _(zz=zz, vxy=vxy, lane=lane, pending=pending):
                    totals = None
                    for half in range(2):
                        space_unit(t, zz, lane, half, vall, vxy, links, field, kets[lane])
                        totals = plus(totals, space_product(*pending, half, vall, kets[pending[2]]))
                    for half in range(2):
                        acc_s[pending[0], half] += totals[half]
                    if zz == 0:
                        shift_half(t, 1, vxy_b, lane)
                    else:
                        shift_half(jnp.minimum(t + 1, 1), 0, vxy_a, lane)

                pending = (t, zz, lane)
        return 0

    lax.fori_loop(0, 2, blocks, 0)
    for chunk in range(2):
        for half, part in enumerate(space_product(1, 1, 1, chunk, vall, ket_s1)):
            acc_s[1, half] += part

    def spread_edge(number, slot, mu):
        for entry in range(18):
            links[slot, mu * 18 + entry] = jnp.broadcast_to(
                edge_in[number, entry : entry + 1], (8, SITES)
            )
        field[slot, mu] = jnp.broadcast_to(edge_in[number, 18:19], (8, SITES))

    z_first = jnp.where(x == 0, 0, 1)

    def place(number, which):
        z_t = z_first if which == 0 else 1 - z_first
        is_z = number == 3
        low_t = lax.rem(number + 1, 3)
        low = (jnp.where(is_z, z_t + 1, low_t), jnp.where(is_z, 2 - 2 * z_t, which + 1))
        up = (jnp.where(is_z, z_t + 1, low_t + 1), jnp.where(is_z, 3 - 2 * z_t, which + 1))
        slot = jnp.where(
            is_z, 1 + 3 * z_t, jnp.where(number == 2, 5, number * 2) + which
        )
        product = number * 2 + jnp.where(is_z, z_t, which)
        sign = jnp.where(is_z, -1.0, 1.0).astype(jnp.bfloat16)
        return low, up, slot, product, sign, z_t

    def product_of(number, which, ket, units=None):
        low, _, _, product, sign, _ = place(number, which)
        totals = None
        for chunk in range(4):
            if units is not None:
                units(chunk)
            totals = plus(totals, link_product(low, sign, chunk, vall, ket))
        for half in range(2):
            acc_p[product, half] = totals[half]

    def pair(number, previous):
        is_z = number == 3
        active = jnp.logical_or(
            jnp.logical_or(number == 0, is_z),
            jnp.logical_or(
                jnp.logical_and(number == 1, upper_down), jnp.logical_and(number == 2, lower_up)
            ),
        )

        @pl.when(active)
        def _():
            for which, ket in enumerate((ket_p0, ket_p1)):
                _, up, slot, _, _, z_t = place(number, which)

                @pl.when(number == 1)
                def _():
                    arrive(down_t[which])

                @pl.when(number == 2)
                def _():
                    arrive(up_t[which])
                    if which == 0:
                        arrive(edge_t)

                    @pl.when(lower_up)
                    def _():
                        spread_edge(1 + which, 5 + which, 3)

                @pl.when(jnp.logical_and(is_z, z_t == 0))
                def _():
                    arrive(down_z)

                @pl.when(jnp.logical_and(is_z, z_t == 1))
                def _():
                    arrive(up_z)
                    arrive(edge_z)
                    spread_edge(0, 4, 2)

                mu = jnp.where(is_z, 2, 3)

                def units(step, up=up, slot=slot, ket=ket):
                    link_unit(up, slot, mu, step // 2, step % 2, vall, links, field, ket)

                if which == 0:
                    product_of(previous, 1, ket_p1, units)
                else:
                    product_of(number, 0, ket_p0, units)

        return jnp.where(active, number, previous)

    lax.fori_loop(0, 4, pair, jnp.int32(0))
    product_of(jnp.int32(3), 1, ket_p1)

    own[4].wait()
    begin = start_ref[0]
    lattice_t = 2 * n_ta

    def inside(t):
        offset = (ta * 2 + t - begin + 2 * lattice_t) % lattice_t
        return jnp.where(offset < TW, 1.0, 0.0)

    before, first_in, last_in, after = (inside(t) for t in (-1, 0, 1, 2))

    def by_part(values, groups):
        rows = []
        for group in range(groups):
            for part in range(2):
                base = group * 32 + part * 8
                rows.append(
                    jnp.concatenate([values[base : base + 8], values[base + 16 : base + 24]], axis=0)
                )
        return jnp.concatenate(rows, axis=1)

    def both(acc, index):
        return jnp.concatenate([acc[index, 0], acc[index, 1]], axis=1)

    spaces = [by_part(both(acc_s, t), 1) for t in range(2)]
    times_in, times_up, times_low = (
        by_part(both(acc_p, 2 * number) + both(acc_p, 2 * number + 1), 2) for number in range(3)
    )
    z_links = [by_part(both(acc_p, 6 + t), 2) for t in range(2)]
    space_in = first_in * spaces[0] + last_in * spaces[1]
    z_in = first_in * z_links[0] + last_in * z_links[1]
    products = jnp.concatenate(
        [
            jnp.concatenate(
                [spaces[0] + spaces[1], times_in + times_up + times_low, z_links[0] + z_links[1]],
                axis=1,
            ),
            jnp.concatenate(
                [
                    space_in,
                    first_in * times_in + last_in * times_up + before * times_low,
                    z_in,
                ],
                axis=1,
            ),
            jnp.concatenate(
                [
                    space_in,
                    last_in * times_in + after * times_up + first_in * times_low,
                    z_in,
                ],
                axis=1,
            ),
        ],
        axis=0,
    )
    own[3].wait()
    own[5].wait()
    high, rest = split(products)
    middle, low = split(products - high.astype(jnp.float32))
    folded = jnp.dot(
        jnp.concatenate([high, middle, low], axis=0),
        table[...],
        preferred_element_type=jnp.float32,
    )
    folded = folded[:48] + folded[48:96] + folded[96:]
    lane = lax.broadcasted_iota(jnp.int32, (1, 128), 1)
    windowed = jnp.where(lane < 64, folded[16:32], folded[32:])
    backward = jnp.transpose(jnp.concatenate([folded[:16], windowed], axis=0))[64:]
    pieces = [
        backward[group * 16 : group * 16 + 16, window * 16 : window * 16 + 16]
        for window in range(2)
        for group in range(4)
    ]
    value = jnp.concatenate([folded[:16, :64], windowed[:, :64]], axis=1)
    value = value + jnp.concatenate(pieces, axis=1)

    if comm:

        def message(src, number, slot, sent, device):
            return pltpu.make_async_remote_copy(
                src_ref=src,
                dst_ref=slots.at[number, slot],
                send_sem=sum_send.at[sent],
                recv_sem=sum_recv.at[number, slot],
                device_id=device,
                device_id_type=MESH,
            )

        def gather(number, found, last):
            for slot, device in found:
                message(slots.at[number, slot], number, slot, 0, device).wait_recv()
            total = slots[number, 0]
            for other in range(1, last):
                total = total + slots[number, other]
            return total

        @pl.when(is_first)
        def _():
            share[...] = value
            started = [
                message(share, 0, 4 + x, step, device)
                for step, (_, device) in enumerate(along_row)
            ]
            for copy in started:
                copy.start()
            whole[...] = gather(2, along_column, 8)
            for copy in started:
                copy.wait_send()

        @pl.when(is_second)
        def _():
            total = value
            started = []
            for number, (others, index) in enumerate(stages):
                slots[number, index] = total
                targets = [(index, device) for _, device in others]
                if number == 2:
                    firsts = [(index, device) for _, device in along_column]
                    pairs = zip(firsts[:-1], targets)
                    targets = [target for two in pairs for target in two] + firsts[-1:]
                for slot, device in targets:
                    copy = message(slots.at[number, index], number, slot, len(started), device)
                    copy.start()
                    started.append(copy)
                found = list(others)
                if number == 0:
                    found += [(4 + place_x, device) for place_x, device in along_row]
                total = gather(number, found, 8)
            whole[...] = total
            for copy in started:
                copy.wait_send()

        value = whole[...]
        for item in (down_z, up_z, *down_t, *up_t, edge_z, edge_t):
            guarded(item[1], item[0].wait_send)

    charge = jnp.zeros((1, 128), jnp.float32)
    for mode in range(MODES):
        charge = jnp.where(lane % 16 == mode, charge_ref[mode].astype(jnp.float32), charge)
    charge = charge / 3.0
    volume = 24.0 * SITES * (2 * n_gz)
    scale = jnp.where(
        lane < 64, 1.0 / math.sqrt(volume * lattice_t), 1.0 / math.sqrt(volume * TW)
    )
    scale = scale * jnp.where(lane // 16 % 2 == 0, charge, charge * charge)
    out_ref[...] = value * scale


def insert_sums(counts, comm, low, links, photon, charges, start):
    vmem = pl.BlockSpec(memory_space=pltpu.VMEM)
    return pl.pallas_call(
        functools.partial(hop_kernel, counts, comm),
        out_shape=pltpu.VMEM((MODES, 128), jnp.float32),
        in_specs=[pl.BlockSpec(memory_space=pl.ANY)] * 6,
        out_specs=vmem,
        scratch_shapes=[
            pltpu.SMEM(start.shape, start.dtype),
            pltpu.SMEM(charges.shape, charges.dtype),
            pltpu.VMEM(low.shape, low.dtype),
            pltpu.VMEM(links.shape, links.dtype),
            pltpu.VMEM(photon.shape, photon.dtype),
            pltpu.VMEM((1536, 128), jnp.bfloat16),
            pltpu.VMEM((4, 4, SC, 32, SITES), jnp.bfloat16),
            pltpu.VMEM((ROWS, 2 * SITES), jnp.float32),
            pltpu.VMEM((ROWS, 2 * SITES), jnp.float32),
            pltpu.VMEM((SITES, 2 * SITES), jnp.bfloat16),
            pltpu.VMEM((7, 72, 8, SITES), jnp.float32),
            pltpu.VMEM((7, 4, 8, SITES), jnp.float32),
            pltpu.VMEM((3, EDGE, SITES), jnp.float32),
            pltpu.VMEM((3, EDGE, SITES), jnp.float32),
            pltpu.VMEM((256, SC * 128), jnp.bfloat16),
            pltpu.VMEM((256, SC * 128), jnp.bfloat16),
            pltpu.VMEM((128, SC * SITES), jnp.bfloat16),
            pltpu.VMEM((128, SC * SITES), jnp.bfloat16),
            pltpu.VMEM((2, 2, 32, 128), jnp.float32),
            pltpu.VMEM((8, 2, 64, 64), jnp.float32),
            pltpu.VMEM((MODES, 128), jnp.float32),
            pltpu.VMEM((3, 8, MODES, 128), jnp.float32),
            pltpu.VMEM((MODES, 128), jnp.float32),
            pltpu.SemaphoreType.DMA((6,)),
            pltpu.SemaphoreType.DMA((8,)),
            pltpu.SemaphoreType.DMA((8,)),
            pltpu.SemaphoreType.DMA((25,)),
            pltpu.SemaphoreType.DMA((3, 8)),
        ],
        compiler_params=pltpu.CompilerParams(
            collective_id=0 if comm else None,
            has_side_effects=comm,
            vmem_limit_bytes=60 * 1024 * 1024,
        ),
    )(start, charges, low, links, photon, jnp.asarray(fold_table(), jnp.bfloat16))


def lay_out(sums, *outputs):
    for window in range(2):
        for part in range(2):
            for order in range(2):
                start = window * 64 + part * 32 + order * 16
                outputs[window * 2 + order][part] = sums[:, start : start + 16]


def per_device(counts, comm, low_modes, gauge_links, photon, charges, window_start):
    sums = insert_sums(counts, comm, low_modes, gauge_links, photon, charges, window_start)
    vmem = pl.BlockSpec(memory_space=pltpu.VMEM)
    return pl.pallas_call(
        lay_out,
        out_shape=[jax.ShapeDtypeStruct((2, MODES, MODES), jnp.float32)] * 4,
        in_specs=[vmem],
        out_specs=[vmem] * 4,
        compiler_params=pltpu.CompilerParams(vmem_limit_bytes=1024 * 1024),
    )(sums)


def solution(mesh):
    counts = (mesh.shape["gz"], mesh.shape["ta"])
    return jax.shard_map(
        functools.partial(per_device, counts, True),
        mesh=mesh,
        in_specs=(
            P(None, None, None, None, "ta", "gz", None),
            P(None, None, "ta", "gz", None),
            P(None, "ta", "gz", None),
            P(),
            P(),
        ),
        out_specs=(P(), P(), P(), P()),
        check_vma=False,
    )
```
